32 devices in a mesh: batch: 8 (over z, y), head: 4 (over x, core).
Axes of the slice: x: 2, y: 2, z: 4, core: 2. Of those that a mesh axis runs over, the one named last changes fastest.
Arguments:
- residual: float32 [8192, 768], P('batch'), may hold values from -6 to 6
- cotangent: float32 [8192, 768], P('batch'), may hold values from -6 to 6
- lengths: int32 [8], P('batch'), may hold values from 1 to 1024, as said below
- gains: float32 [2, 768], replicated, may hold values from 0.5 to 1.5
- heads_weight: float32 [768, 3, 768], P(None, None, 'head'), may hold values from -0.21875 to 0.21875
- merge_weight: float32 [768, 768], P('head'), may hold values from -4 to 4
- expand_weight: float32 [768, 3072], P(None, 'head'), may hold values from -0.21875 to 0.21875
- shrink_weight: float32 [3072, 768], P('head'), may hold values from -0.109375 to 0.109375
- gain_moment: float32 [2, 768], replicated, may hold values from 409.6 to 8192
- heads_rows: float32 [768], P('batch'), may hold values from 655.36 to 5734.4
- heads_cols: float32 [3, 768], P(None, 'head'), may hold values from 655.36 to 5734.4
- merge_rows: float32 [768], P('head'), may hold values from 1.92 to 16
- merge_cols: float32 [768], P('batch'), may hold values from 1.92 to 16
- expand_rows: float32 [768], P('batch'), may hold values from 57.344 to 491.52
- expand_cols: float32 [3072], P('head'), may hold values from 57.344 to 491.52
- shrink_rows: float32 [3072], P('head'), may hold values from 245.76 to 2293.76
- shrink_cols: float32 [768], P('batch'), may hold values from 245.76 to 2293.76
Outputs:
- block_out: float32 [8192, 768], P('batch')
- residual_grad: float32 [8192, 768], P('batch')
- heads_grad: float32 [768, 3, 768], P('batch', None, 'head')
- heads_rows_next: float32 [768], P('batch')
- heads_cols_next: float32 [3, 768], P(None, 'head')
- heads_weight_next: float32 [768, 3, 768], P('batch', None, 'head')
- merge_grad: float32 [768, 768], P('head', 'batch')
- merge_rows_next: float32 [768], P('head')
- merge_cols_next: float32 [768], P('batch')
- merge_weight_next: float32 [768, 768], P('head', 'batch')
- expand_grad: float32 [768, 3072], P('batch', 'head')
- expand_rows_next: float32 [768], P('batch')
- expand_cols_next: float32 [3072], P('head')
- expand_weight_next: float32 [768, 3072], P('batch', 'head')
- shrink_grad: float32 [3072, 768], P('head', 'batch')
- shrink_rows_next: float32 [3072], P('head')
- shrink_cols_next: float32 [768], P('batch')
- shrink_weight_next: float32 [3072, 768], P('head', 'batch')
- gains_grad: float32 [2, 768], replicated
- gain_moment_next: float32 [2, 768], replicated
- gains_next: float32 [2, 768], replicated
- update_rms: float32 [], replicated
The draws below stay inside these ranges and needn't reach their ends.
Inputs may be any that keep to these rules, and one draw needn't show every extreme that they name: Live lengths of the sequences; one sequence, drawn from the seed, is full.
All inputs are finite; a program needn't handle non-finite values.
Results may differ from the reference program's by a relative error of at most 0.012.
The reference program's roundings to bfloat16 on the way count: a program that leaves them out, or rounds other values in their place, can miss the bound.
Values sent between devices are 32-bit elements; how exact they have to be, the bound alone decides.
A program may use at most 128 MiB of HBM per device.

```python
import math
import jax
import jax.numpy as jnp
from jax import lax

D = 768
HEADS = 12
HEAD_DIM = 64
FF = 3072
SEQ_LEN = 1024
STEP = 10
SEQS = 8
TOKENS = 8192


def draw_lengths(key, part):
    key = jax.random.fold_in(key, 11)
    first_key, second_key = jax.random.split(key)
    order = jnp.arange(SEQS, dtype=jnp.int32)
    base_len = SEQ_LEN // 3 + 2 * SEQ_LEN // 3 * order // max(SEQS - 1, 1)
    jitter = jax.random.randint(first_key, (SEQS,), 0, SEQ_LEN // 8 + 1, dtype=jnp.int32)
    lengths = jnp.clip(base_len - jitter, 1, SEQ_LEN)
    chosen = jax.random.randint(second_key, (), 0, SEQS, dtype=jnp.int32)
    lengths = jnp.where(order == chosen, SEQ_LEN, lengths)
    return lengths.astype(jnp.int32)


def steps_of(own_key, dims, cuts, smallest, largest):
    loudness = 1.0
    for position, shards_of in cuts:
        heights = jax.random.uniform(jax.random.fold_in(jax.random.fold_in(own_key, 6), position), (shards_of,), jnp.float32, smallest / len(cuts), largest / len(cuts))
        loudness = loudness * jnp.repeat(jnp.exp(heights), dims[position] // shards_of).reshape((-1,) + (1,) * (len(dims) - 1 - position))
    return loudness


def centred(own_key, extent, spread, most, cuts=(), held_as=jnp.bfloat16):
    factor_of = steps_of(own_key, extent, cuts, -0.22, 0.18) if cuts else 1.0
    drawn = jax.random.normal(own_key, extent, jnp.float32) * spread * factor_of
    return jnp.minimum(jnp.maximum(drawn, -most), most).astype(held_as)


def setup_inputs(seed: int = 0) -> dict:
    streams_of = jax.random.split(jax.random.key(seed), 18)
    return {
        "residual": centred(streams_of[0], (TOKENS, D), 1.0, 6.0, ((0, 8),), jnp.float32),
        "cotangent": centred(streams_of[1], (TOKENS, D), 1.0, 6.0, ((0, 8),), jnp.float32),
        "lengths": draw_lengths(jax.random.fold_in(streams_of[17], 71), 0),
        "gains": jnp.clip(1.0 + 0.1 * jax.random.normal(streams_of[3], (2, D), jnp.float32), 0.5, 1.5),
        "heads_weight": centred(streams_of[4], (D, 3, D), D ** -0.5, 0.21875, ((2, 4),), jnp.float32),
        "merge_weight": centred(streams_of[5], (D, D), (max(1, 3 * D // SEQ_LEN)) ** -0.5, 4.0, ((0, 4),), jnp.float32),
        "expand_weight": centred(streams_of[6], (D, FF), D ** -0.5, 0.21875, ((1, 4),), jnp.float32),
        "shrink_weight": centred(streams_of[7], (FF, D), FF ** -0.5, 0.109375, ((0, 4),), jnp.float32),
        "gain_moment": jnp.clip(jnp.exp(jax.random.uniform(streams_of[8], (2, D), jnp.float32, math.log(409.6), math.log(8192.0))), 409.6, 8192.0),
        "heads_rows": jnp.clip(jnp.exp(math.log(5734.4) - 2.1690537 * jax.random.uniform(streams_of[9], (D,), jnp.float32) ** steps_of(streams_of[9], (D,), ((0, 8),), -0.2, 0.2)), 655.36, 5734.4),
        "heads_cols": jnp.clip(jnp.exp(math.log(5734.4) - 2.1690537 * jax.random.uniform(streams_of[10], (3, D), jnp.float32) ** steps_of(streams_of[10], (3, D), ((1, 4),), -0.2, 0.2)), 655.36, 5734.4),
        "merge_rows": jnp.clip(jnp.exp(math.log(16.0) - 2.1202636 * jax.random.uniform(streams_of[11], (D,), jnp.float32) ** steps_of(streams_of[11], (D,), ((0, 4),), -0.2, 0.2)), 1.92, 16.0),
        "merge_cols": jnp.clip(jnp.exp(math.log(16.0) - 2.1202636 * jax.random.uniform(streams_of[12], (D,), jnp.float32) ** steps_of(streams_of[12], (D,), ((0, 8),), -0.2, 0.2)), 1.92, 16.0),
        "expand_rows": jnp.clip(jnp.exp(math.log(491.52) - 2.1484344 * jax.random.uniform(streams_of[13], (D,), jnp.float32) ** steps_of(streams_of[13], (D,), ((0, 8),), -0.2, 0.2)), 57.344, 491.52),
        "expand_cols": jnp.clip(jnp.exp(math.log(491.52) - 2.1484344 * jax.random.uniform(streams_of[14], (FF,), jnp.float32) ** steps_of(streams_of[14], (FF,), ((0, 4),), -0.2, 0.2)), 57.344, 491.52),
        "shrink_rows": jnp.clip(jnp.exp(math.log(2293.76) - 2.2335922 * jax.random.uniform(streams_of[15], (FF,), jnp.float32) ** steps_of(streams_of[15], (FF,), ((0, 4),), -0.2, 0.2)), 245.76, 2293.76),
        "shrink_cols": jnp.clip(jnp.exp(math.log(2293.76) - 2.2335922 * jax.random.uniform(streams_of[16], (D,), jnp.float32) ** steps_of(streams_of[16], (D,), ((0, 8),), -0.2, 0.2)), 245.76, 2293.76),
    }


highest = lax.Precision.HIGHEST
tiny_term = 1e-30
clip_level = 0.5

@jax.custom_vjp
def low(v):
    return lax.optimization_barrier(v.astype(jnp.bfloat16)).astype(jnp.float32)

@jax.custom_vjp
def low_back(v):
    return v

def low_keep(v):
    return (low(v), None)

def low_pass(kept, grad):
    return (grad,)

def back_keep(v):
    return (v, None)

def back_low(kept, grad):
    return (low(grad),)
low.defvjp(low_keep, low_pass)
low_back.defvjp(back_keep, back_low)

def norm_rows(values, gain):
    center = values - lax.optimization_barrier(jnp.mean(values, -1, keepdims=True))
    variance = lax.optimization_barrier(jnp.mean(center * center, -1, keepdims=True))
    return center * lax.rsqrt(variance + 1e-05) * gain

def attend(queries, key_rows, value_rows, length):
    block_rows = min(512, SEQ_LEN)
    block_count = SEQ_LEN // block_rows
    positions = jnp.arange(SEQ_LEN, dtype=jnp.int32)
    starts = jnp.arange(block_count, dtype=jnp.int32) * block_rows
    blocks = queries.reshape(block_count, block_rows, HEADS, HEAD_DIM)

    def one_block(block_pair):
        query_blk, block_start = block_pair
        scores = low_back(jnp.einsum('qhd,khd->hqk', query_blk, key_rows, precision=highest) * HEAD_DIM ** (-0.5))
        row_index = block_start + jnp.arange(block_rows, dtype=jnp.int32)
        allowed = (positions[None, :] <= row_index[:, None]) & (positions[None, :] < length)
        soft_abs = jnp.sqrt(scores * scores + 1.0)
        masked = jnp.where(allowed[None], soft_abs, -jnp.inf)
        row_top = lax.optimization_barrier(jnp.max(masked, -1, keepdims=True))
        exponent = jnp.exp(masked - row_top)
        weights = exponent / lax.optimization_barrier(jnp.sum(exponent, -1, keepdims=True))
        probs = low(jnp.tanh(scores) * weights)
        return jnp.einsum('hqk,khd->qhd', probs, value_rows, precision=highest)
    mixed = lax.map(jax.checkpoint(one_block), (blocks, starts))
    return mixed.reshape(SEQ_LEN, HEADS * HEAD_DIM)

def layer(values, gains, heads_weight, merge_weight, expand_weight, shrink_weight, length):
    first = low(norm_rows(values, gains[0]))
    joint_rows = jnp.dot(first, low(heads_weight).reshape(D, 3 * D), precision=highest)
    joint_rows = low_back(low(joint_rows)).reshape(SEQ_LEN, 3, HEADS, HEAD_DIM)
    attended = attend(joint_rows[:, 0], joint_rows[:, 1], joint_rows[:, 2], length)
    attended = low_back(low(attended))
    middle = values + low_back(jnp.dot(attended, low(merge_weight), precision=highest))
    second = low(norm_rows(middle, gains[1]))
    expanded = low_back(jnp.dot(second, low(expand_weight), precision=highest))
    activated = low(jax.nn.gelu(expanded, approximate=True))
    return middle + low_back(jnp.dot(activated, low(shrink_weight), precision=highest))

def factored(gradient, row_old, col_old, beta):
    squared = gradient * gradient
    row_next = beta * row_old + (1.0 - beta) * (lax.optimization_barrier(jnp.mean(squared, 1)) + tiny_term)
    col_next = beta * col_old + (1.0 - beta) * (lax.optimization_barrier(jnp.mean(squared, 0)) + tiny_term)
    update = gradient * lax.rsqrt(row_next[:, None] * col_next[None, :] / jnp.mean(row_next))
    return (row_next, col_next, update)

def reference(residual, cotangent, lengths, gains, heads_weight, merge_weight, expand_weight, shrink_weight, gain_moment, heads_rows, heads_cols, merge_rows, merge_cols, expand_rows, expand_cols, shrink_rows, shrink_cols):
    live_rows = (jnp.arange(SEQ_LEN, dtype=jnp.int32)[None, :] < lengths[:, None]).astype(jnp.float32)
    seq_inputs = residual.reshape(SEQS, SEQ_LEN, D)
    seq_cots = cotangent.reshape(SEQS, SEQ_LEN, D) * live_rows[:, :, None]
    params = (gains, heads_weight, merge_weight, expand_weight, shrink_weight)

    def one_sequence(running, seq_item):
        seq_in, seq_cot, length = seq_item

        def forward(seq_values, gain_vals, heads_vals, merge_vals, expand_vals, shrink_vals):
            return layer(seq_values, gain_vals, heads_vals, merge_vals, expand_vals, shrink_vals, length)
        seq_out, pull = jax.vjp(forward, seq_in, *params)
        pulled = pull(seq_cot)
        running = tuple((before + fresh for before, fresh in zip(running, pulled[1:])))
        return (running, (seq_out, pulled[0]))
    start_sums = tuple((jnp.zeros_like(param) for param in params))
    sums, (outputs, input_grads) = lax.scan(one_sequence, start_sums, (seq_inputs, seq_cots, lengths))
    gains_grad, heads_grad, merge_grad, expand_grad, shrink_grad = sums
    beta = 1.0 - STEP ** (-0.8)
    heads_rows_next, heads_cols_flat, heads_update = factored(heads_grad.reshape(D, 3 * D), heads_rows, heads_cols.reshape(3 * D), beta)
    merge_rows_next, merge_cols_next, merge_update = factored(merge_grad, merge_rows, merge_cols, beta)
    expand_rows_next, expand_cols_next, expand_update = factored(expand_grad, expand_rows, expand_cols, beta)
    shrink_rows_next, shrink_cols_next, shrink_update = factored(shrink_grad, shrink_rows, shrink_cols, beta)
    gain_moment_next = beta * gain_moment + (1.0 - beta) * (gains_grad * gains_grad + tiny_term)
    gain_step = gains_grad * lax.rsqrt(gain_moment_next)
    squares = jnp.sum(heads_update * heads_update) + jnp.sum(merge_update * merge_update) + jnp.sum(expand_update * expand_update) + jnp.sum(shrink_update * shrink_update) + jnp.sum(gain_step * gain_step)
    update_rms = jnp.sqrt(squares / (4.0 * D * D + 2.0 * D * FF + 2.0 * D))
    clip = 1.0 / jnp.maximum(1.0, update_rms / clip_level)

    def renew(weight, update):
        return weight - jnp.sqrt(jnp.mean(weight * weight)) * clip * update
    heads_weight_next = renew(heads_weight, heads_update.reshape(D, 3, D))
    merge_weight_next = renew(merge_weight, merge_update)
    expand_weight_next = renew(expand_weight, expand_update)
    shrink_weight_next = renew(shrink_weight, shrink_update)
    gains_next = gains - jnp.sqrt(lax.optimization_barrier(jnp.mean(gains * gains, 1, keepdims=True))) * clip * gain_step
    return (outputs.reshape(TOKENS, D), input_grads.reshape(TOKENS, D), heads_grad, heads_rows_next, heads_cols_flat.reshape(3, D), heads_weight_next, merge_grad, merge_rows_next, merge_cols_next, merge_weight_next, expand_grad, expand_rows_next, expand_cols_next, expand_weight_next, shrink_grad, shrink_rows_next, shrink_cols_next, shrink_weight_next, gains_grad, gain_moment_next, gains_next, update_rms)
```

```python
from functools import partial

import jax
import jax.numpy as jnp
from jax import lax
from jax.experimental import pallas as pl
from jax.experimental.pallas import tpu as pltpu
from jax.sharding import PartitionSpec as P

HEAD_DIM = 64
FF = 3072
STEP = 10
CHUNK = 256

tiny_term = 1e-30
clip_level = 0.5
f32 = jnp.float32
bf16 = jnp.bfloat16
LOG2E = 1.4426950408889634
GELU_A = 0.7978845608028654
GELU_B = 0.044715
MESH = pl.DeviceIdType.MESH
VMEM_LIMIT = 63 * 1024 * 1024


def mm(a, b):
    return jnp.dot(a, b, preferred_element_type=f32)


def mm_nt(a, b):
    return lax.dot_general(a, b, (((1,), (1,)), ((), ())), preferred_element_type=f32)


def mm_tn(a, b):
    return lax.dot_general(a, b, (((0,), (0,)), ((), ())), preferred_element_type=f32)


def identity(size):
    rows = lax.broadcasted_iota(jnp.int32, (size, size), 0)
    return (rows == lax.broadcasted_iota(jnp.int32, (size, size), 1)).astype(bf16)


def band(start, size):
    return pl.ds(pl.multiple_of(start, size), size)


def tiles(total, rows, body):
    def step(i, carry):
        body(i * rows)
        return carry

    lax.fori_loop(0, total // rows, step, 0)


def cast_rows(src, dst, rows=64):
    def one(at):
        dst[band(at, rows), :] = src[band(at, rows), :].astype(bf16)

    tiles(src.shape[0], rows, one)


def fold(values, how):
    groups = values.reshape(values.shape[0] // 8, 8, values.shape[1])
    return how(groups, 0)


def normalize(values):
    center = values - jnp.mean(values, -1, keepdims=True)
    inv_dev = lax.rsqrt(jnp.mean(center * center, -1, keepdims=True) + 1e-05)
    return center * inv_dev, inv_dev


def norm_back(upstream, gain, normed, inv_dev):
    scaled = upstream * gain
    inner = (
        scaled
        - jnp.mean(scaled, -1, keepdims=True)
        - normed * jnp.mean(scaled * normed, -1, keepdims=True)
    )
    return inner * inv_dev


def head_place():
    me = lax.axis_index("head")
    core = lax.rem(me, 2)
    side = me // 2
    return core, side, me + 1 - 2 * core, me + 2 - 4 * side


def greet(peers):
    barrier = pltpu.get_barrier_semaphore()
    for peer in peers:
        pl.semaphore_signal(barrier, inc=1, device_id=peer, device_id_type=MESH)


def await_greetings(count):
    pl.semaphore_wait(pltpu.get_barrier_semaphore(), count)


STEPS = {
    "project": (1, 0, 4, 5),
    "score": (1, 2, 4, 6),
    "weigh": (1, 3, 4, 7),
    "mix": (1, 3, 4, 7),
    "attn_forward": (8, 6, 7, 9),
    "feed": (10, 8, 9, 11),
    "mid_core": (13, 9, 11, 12),
    "mid_chip": (16, 11, 13, 15),
    "back_first": (20, 19, 17, 15),
    "back_second": (20, 19, 17, 16),
    "back_third": (21, 19, 18, 16),
    "in_core": (22, 21, 20, 18),
    "in_chip": (23, 22, 21, 20),
    "out_core": (15, 20, 23, 13),
    "out_chip": (21, 22, 25, 23),
    "merge": (2, 5, 8),
    "cast": (0, 1),
    "clear": 5,
    "wide": (11, 15, 13, 14, 12, 14, 13),
    "pair": (12, 20, 15, 17, 14, 18, 16, 21, 22, 21, 22, 23, 23),
    "rest": (22, 23, 23, 20, 22, 20, 24, 22, 24, 23, 24, 24, 24),
    "update": (24, 25, 25, 25),
    "last_forward": 11,
    "first_backward": 9,
    "all": 26,
}


class Gather:
    def __init__(self, box, sems, axis):
        self.box, self.sems, self.axis = box, sems, axis
        self.count = box.shape[0]
        self.me = lax.axis_index(axis)

    def copy(self, k, slot):
        return pltpu.make_async_remote_copy(
            src_ref=self.box.at[slot],
            dst_ref=self.box.at[slot],
            send_sem=self.sems.at[0, k],
            recv_sem=self.sems.at[1, slot],
            device_id={self.axis: lax.rem(self.me + k, self.count)},
            device_id_type=MESH,
        )

    def each(self, action):
        def step(k, carry):
            action(k)
            return carry

        lax.fori_loop(1, self.count, step, 0)

    def start(self):
        self.each(lambda k: self.copy(k, self.me).start())

    def total(self):
        self.each(lambda k: self.copy(k, lax.rem(self.me + k, self.count)).wait_recv())
        return lax.fori_loop(
            1, self.count, lambda i, running: running + self.box[i], self.box[0]
        )

    def settle(self):
        self.each(lambda k: self.copy(k, self.me).wait_send())


def others(axis, count):
    me = lax.axis_index(axis)
    return [{axis: lax.rem(me + k, count)} for k in range(1, count)]


def pick(lane, values):
    row = jnp.zeros(lane.shape, f32)
    for at, value in enumerate(values):
        row = jnp.where(lane == at, value, row)
    return row


class HeadSum:
    def __init__(self, part, whole, from_core, from_chip, sems, place, home=False, chip_at=0):
        self.part, self.whole, self.home, self.chip_at = part, whole, home, chip_at
        self.from_core, self.from_chip, self.sems = from_core, from_chip, sems
        self.core, self.side, self.sibling, self.across = place

    def copy(self, src, dst, stage, c, peer):
        return pltpu.make_async_remote_copy(
            src_ref=src,
            dst_ref=dst,
            send_sem=self.sems.at[0, stage, c],
            recv_sem=self.sems.at[1, stage, c],
            device_id={"head": peer},
            device_id_type=MESH,
        )

    def pair(self, ref, c):
        return ref.at[pl.ds(2 * c, 2)]

    def mine(self, c):
        return self.whole.at[pl.ds(4 * c + 2 * self.core, 2)]

    def to_core(self, c):
        src = self.part.at[pl.ds(4 * c + 2 * (1 - self.core), 2)]
        return self.copy(src, self.pair(self.from_core, c), 0, c, self.sibling)

    def to_chip(self, c):
        return self.copy(
            self.pair(self.from_core, c),
            self.from_chip.at[pl.ds(self.chip_at + 2 * c, 2)],
            1,
            c,
            self.across,
        )

    def back_core(self, c):
        src = self.pair(self.from_core, c) if self.home else self.mine(c)
        return self.copy(src, self.mine(c), 2, c, self.sibling)

    def keep(self, c):
        return pltpu.make_async_copy(
            self.pair(self.from_core, c), self.mine(c), self.sems.at[0, 3, c]
        )

    def store(self, c, values):
        quarter = self.part.shape[1]
        for i in range(4):
            self.part[4 * c + i] = values[i * quarter : (i + 1) * quarter]

    def start(self, c):
        self.to_core(c).start()

    def reduce_core(self, c):
        self.to_core(c).wait()
        for half in range(2):
            self.from_core[2 * c + half] = (
                self.from_core[2 * c + half] + self.part[4 * c + 2 * self.core + half]
            )
        self.to_chip(c).start()

    def reduce_chip(self, c, finish):
        self.to_chip(c).wait()
        for half in range(2):
            total = self.from_core[2 * c + half] + self.from_chip[self.chip_at + 2 * c + half]
            result = finish(total, c, half)
            if self.home:
                self.from_core[2 * c + half] = result
            else:
                self.whole[4 * c + 2 * self.core + half] = result
        self.back_core(c).start()
        if self.home:
            self.keep(c).start()

    def arrive(self, c):
        self.back_core(c).wait()
        if self.home:
            self.keep(c).wait()


class HeadGather:
    def __init__(self, slot, sems, place):
        self.slot, self.sems = slot, sems
        self.core, self.side, self.sibling, self.across = place
        self.me = 2 * self.side + self.core

    def copy(self, stage, owner, c, peer):
        ref = self.slot(c, owner)
        return pltpu.make_async_remote_copy(
            src_ref=ref,
            dst_ref=ref,
            send_sem=self.sems.at[0, stage, c],
            recv_sem=self.sems.at[1, stage, c],
            device_id={"head": peer},
            device_id_type=MESH,
        )

    def over(self, c):
        return self.copy(0, self.me, c, self.across)

    def beside(self, c):
        return self.copy(1, self.me, c, self.sibling)

    def onward(self, c):
        return self.copy(2, self.across, c, self.sibling)

    def start(self, c):
        self.over(c).start()
        self.beside(c).start()

    def forward(self, c):
        self.over(c).wait_recv()
        self.onward(c).start()

    def arrive(self, c):
        self.over(c).wait_send()
        self.beside(c).wait()
        self.onward(c).wait()


class WeightGather:
    def __init__(self, slot, sems, place):
        self.slot, self.sems = slot, sems
        self.core, self.side, self.sibling, self.across = place
        self.me = 2 * self.side + self.core
        batch = lax.axis_index("batch")
        self.parity = lax.rem(batch, 2)
        self.pair = batch + 1 - 2 * self.parity

    def copy(self, stage, ref, device):
        return pltpu.make_async_remote_copy(
            src_ref=ref,
            dst_ref=ref,
            send_sem=self.sems.at[0, stage, 0],
            recv_sem=self.sems.at[1, stage, 0],
            device_id=device,
            device_id_type=MESH,
        )

    def half(self, owner):
        ref = self.slot(owner)
        columns = ref.shape[2] // 2
        return ref.at[:, :, pl.ds(pl.multiple_of(self.parity * columns, 128), columns)]

    def over(self):
        return self.copy(0, self.half(self.me), {"head": self.across})

    def beside(self):
        return self.copy(1, self.slot(self.me), {"head": self.sibling})

    def onward(self):
        return self.copy(2, self.slot(self.across), {"head": self.sibling})

    def swap(self):
        return self.copy(3, self.half(self.across), {"batch": self.pair})

    def start(self):
        self.over().start()
        self.beside().start()

    def trade(self):
        self.over().wait_recv()
        self.swap().start()

    def forward(self):
        self.swap().wait_recv()
        self.onward().start()

    def arrive(self):
        self.over().wait_send()
        self.swap().wait_send()
        self.beside().wait()
        self.onward().wait()


class BatchScatter:
    def __init__(self, slices, from_pair, from_rest, pair_sems, rest_sems, pieces):
        self.slices, self.from_pair, self.from_rest = slices, from_pair, from_rest
        self.pair_sems, self.rest_sems, self.pieces = pair_sems, rest_sems, pieces
        me = lax.axis_index("batch")
        self.parity, self.place = lax.rem(me, 2), me // 2
        self.pair = me + 1 - 2 * self.parity
        self.count = slices.shape[1]

    def exchange(self, p):
        columns = pl.ds(*self.pieces[p])
        return pltpu.make_async_remote_copy(
            src_ref=self.slices.at[1 - self.parity, :, :, columns],
            dst_ref=self.from_pair.at[:, :, columns],
            send_sem=self.pair_sems.at[0, p],
            recv_sem=self.pair_sems.at[1, p],
            device_id={"batch": self.pair},
            device_id_type=MESH,
        )

    def deliver(self, p, k):
        columns = pl.ds(*self.pieces[p])
        other = lax.rem(self.place + k, self.count)
        return pltpu.make_async_remote_copy(
            src_ref=self.from_pair.at[other, :, columns],
            dst_ref=self.from_rest.at[k - 1, :, columns],
            send_sem=self.rest_sems.at[0, p, k - 1],
            recv_sem=self.rest_sems.at[1, p, k - 1],
            device_id={"batch": other * 2 + self.parity},
            device_id_type=MESH,
        )

    def each(self, p, action):
        def step(k, carry):
            action(self.deliver(p, k))
            return carry

        lax.fori_loop(1, self.count, step, 0)

    def start(self):
        for p in range(len(self.pieces)):
            self.exchange(p).start()

    def reduce_pair(self, p):
        self.exchange(p).wait_recv()
        columns = pl.ds(*self.pieces[p])

        def step(i, carry):
            self.from_pair[i, :, columns] = (
                self.from_pair[i, :, columns] + self.slices[self.parity, i, :, columns]
            )
            return carry

        lax.fori_loop(0, self.count, step, 0)
        self.each(p, lambda copy: copy.start())

    def reduce_rest(self, out, p):
        self.each(p, lambda copy: copy.wait_recv())
        columns = pl.ds(*self.pieces[p])
        out[:, columns] = self.from_pair[self.place, :, columns]

        def step(k, carry):
            out[:, columns] += self.from_rest[k - 1, :, columns]
            return carry

        lax.fori_loop(1, self.count, step, 0)

    def settle(self):
        for p in range(len(self.pieces)):
            self.exchange(p).wait_send()
            self.each(p, lambda copy: copy.wait_send())


def add_slices(ref, half, values):
    count, share = ref.shape[1], ref.shape[2]
    for i in range(count):
        owner = half * count + i
        ref[owner % 2, owner // 2] += values[i * share : (i + 1) * share]


def layer_kernel(
    length_ref,
    gains_ref,
    moment_ref,
    heads_rows,
    heads_cols,
    merge_rows,
    merge_cols,
    expand_rows,
    expand_cols,
    shrink_rows,
    shrink_cols,
    residual_ref,
    cotangent_ref,
    heads_ref,
    merge_ref,
    expand_ref,
    shrink_ref,
    out_ref,
    in_grad_ref,
    heads_own,
    merge_own,
    expand_own,
    shrink_own,
    side_scale,
    lane_scale,
    side_next,
    lane_next,
    gains_grad,
    moment_next,
    gains_next,
    rms_ref,
    gain_one,
    gain_two,
    weight_squares,
    lane_old,
    lane_sum,
    share_sum,
    flat,
    lane_box,
    side_box,
    share_box,
    square_box,
    square_share,
    heads_low,
    merge_low,
    expand_low,
    shrink_low,
    first_ref,
    q_ref,
    k_ref,
    v_ref,
    qt_ref,
    kt_ref,
    vt_ref,
    mixed_ref,
    att_ref,
    logsum_ref,
    middle,
    part,
    mlp_part,
    from_core,
    from_chip,
    mid_chip,
    mlp_sums,
    middle_own,
    second,
    out_low,
    active,
    expand_back,
    second_cols,
    out_cols,
    attended_cols,
    mid_low,
    back_rows,
    back_cols,
    joint_back,
    queries,
    grad_cols,
    query_rows,
    grad_rows,
    row_stats,
    scores,
    probs_low,
    score_low,
    key_sum,
    value_sum,
    query_sum,
    heads_slices,
    merge_slices,
    expand_slices,
    shrink_slices,
    heads_pair,
    heads_rest,
    merge_pair,
    merge_rest,
    expand_pair,
    expand_rest,
    shrink_pair,
    shrink_rest,
    load_sems,
    sum_sems,
    pair_sems,
    rest_sems,
    lane_sems,
    side_sems,
    share_sems,
    square_sems,
    square_share_sems,
):
    chunks, rows, width = first_ref.shape
    quarter = rows // 4
    local = q_ref.shape[2]
    heads = local // HEAD_DIM
    last = chunks - 1
    place = head_place()
    core = place[0]
    me = 2 * place[1] + core

    def merge_slot(owner):
        count = merge_ref.shape[0]
        return middle.at[pl.ds(4 + count * owner, count)]

    merge_gather = WeightGather(merge_slot, sum_sems.at[4], place)
    mixed_gather = HeadGather(
        lambda c, owner: mixed_ref.at[4 * c + owner], sum_sems.at[0], place
    )
    mid_sum = HeadSum(part, middle, from_core, mid_chip, sum_sems.at[1], place)
    in_sum = HeadSum(part, in_grad_ref, from_core, from_chip, sum_sems.at[2], place, True)
    out_sum = HeadSum(
        mlp_part, out_ref, mlp_sums, mlp_sums, sum_sems.at[3], place, True, 2 * chunks
    )
    third = expand_slices.shape[3] // 3
    shrink_pieces = tuple((i * third, third) for i in range(3))
    expand_pieces = shrink_pieces[:2] + tuple((2 * third + i * third // 2, third // 2) for i in range(2))
    heads_pieces = tuple((at, min(128, 3 * local - at)) for at in range(0, 3 * local, 128))
    scatters = [
        BatchScatter(s, p, r, pair_sems.at[i], rest_sems.at[i], pieces)
        for i, (s, p, r, pieces) in enumerate(
            (
                (shrink_slices, shrink_pair, shrink_rest, shrink_pieces),
                (expand_slices, expand_pair, expand_rest, expand_pieces),
                (merge_slices, merge_pair, merge_rest, ((0, local),)),
                (heads_slices, heads_pair, heads_rest, heads_pieces),
            )
        )
    ]
    shrink_scatter, expand_scatter, merge_scatter, heads_scatter = scatters

    def load(src, dst, i):
        return pltpu.make_async_copy(src, dst, load_sems.at[i])

    def load_rows(c):
        return load(residual_ref.at[pl.ds(4 * c, 4)], part.at[pl.ds(4 * c, 4)], c)

    def load_cotangent(c):
        return load(
            cotangent_ref.at[pl.ds(4 * c, 4)], mlp_part.at[pl.ds(4 * c, 4)], chunks + c
        )

    def load_own(c):
        src = residual_ref.at[pl.ds(4 * c + 2 * core, 2)]
        return load(src, mid_chip.at[pl.ds(2 * c, 2)], 2 * chunks + c)

    run = 2 * chunks - 2

    def load_weight(src, i):
        count = src.shape[0]
        spans = ((0, 2, run), (run, 2 * chunks + 2, count - run))
        return [
            load(src.at[pl.ds(at, n)], mlp_sums.at[pl.ds(to, n)], 3 * chunks + 2 * i + half)
            for half, (at, to, n) in enumerate(spans)
        ]

    load_heads, load_expand, load_shrink = (
        load_weight(src, i) for i, src in enumerate((heads_ref, expand_ref, shrink_ref))
    )
    load_merge = load(merge_ref, merge_slot(me), 3 * chunks + 6)

    def start_all(copies):
        for copy in copies:
            copy.start()

    def wait_all(copies):
        for copy in copies:
            copy.wait()

    def each_chunk(action):
        def step(c, carry):
            action(c)
            return carry

        lax.fori_loop(0, chunks, step, 0)

    load_merge.start()
    start_all(load_heads)

    def open_loads(c):
        load_rows(c).start()
        load_cotangent(c).start()

    each_chunk(open_loads)
    share = heads_own.shape[0]
    deep = active.shape[0] > rows
    batch_count, head_count = lane_box.shape[0], side_box.shape[0]
    peers = others("batch", batch_count) + others("head", head_count)
    greet(peers)

    def cast_blocks(count, low, which):
        weight_squares[which] = jnp.zeros(weight_squares.shape[1:], f32)

        def step(i, carry):
            block = mlp_sums[2 + i + 2 * (i // run)]
            low[band(i * quarter, quarter), :] = block.astype(bf16)
            weight_squares[which] += fold(block * block, jnp.sum)
            return carry

        lax.fori_loop(0, count, step, 0)

    wait_all(load_heads)
    cast_blocks(heads_ref.shape[0], heads_low, 0)
    start_all(load_expand)
    load_merge.wait()
    await_greetings(len(peers))
    merge_gather.start()
    length = length_ref[0]
    gain_in, gain_mid = gains_ref[0:1, :], gains_ref[1:2, :]
    eye_local, eye_rows = identity(local), identity(rows)
    head_row = lax.broadcasted_iota(jnp.int32, (local, 1), 0) // HEAD_DIM
    head_col = lax.broadcasted_iota(jnp.int32, (1, local), 1) // HEAD_DIM
    key_row = lax.broadcasted_iota(jnp.int32, (rows, 1), 0)
    gain_one[...] = jnp.zeros_like(gain_one)
    gain_two[...] = jnp.zeros_like(gain_two)

    def live_rows(at, count):
        return (at + lax.broadcasted_iota(jnp.int32, (count, 1), 0) < length).astype(f32)

    def project(c):
        load_rows(c).wait()

        def norm_tile(at):
            values = part[4 * c + at // quarter, band(lax.rem(at, quarter), 64), :]
            first_ref[c, band(at, 64), :] = (normalize(values)[0] * gain_in).astype(bf16)

        tiles(rows, 64, norm_tile)
        normed = first_ref[c]
        live = live_rows(c * rows, rows)
        for which, (row_ref, col_ref) in enumerate(((q_ref, qt_ref), (k_ref, kt_ref), (v_ref, vt_ref))):
            joint = mm_nt(normed, heads_low[which * local : (which + 1) * local, :]).astype(bf16)
            scale = HEAD_DIM ** (-0.5) if which == 0 else live
            joint = (joint.astype(f32) * scale).astype(bf16)
            row_ref[c] = joint
            col_ref[c] = mm_nt(eye_local, joint).astype(bf16)

    def limit_of(c):
        return jnp.minimum(
            c * rows + lax.broadcasted_iota(jnp.int32, (1, rows), 1), length - 1
        )

    def attend_score(c):
        for h in range(heads):
            queries[h] = jnp.where(head_row == h, qt_ref[c].astype(f32), 0.0).astype(bf16)

        def score(kb, tops, limit=None):
            fresh = []
            for h in range(heads):
                s = mm(k_ref[kb], queries[h])
                scores[h, band(kb * rows, rows), :] = s
                square = s * s
                if limit is not None:
                    square = jnp.where(key_row + kb * rows <= limit, square, 0.0)
                fresh.append(jnp.maximum(tops[h], fold(square, jnp.max)))
            return tuple(fresh)

        tops = lax.fori_loop(0, c, score, (jnp.zeros((8, rows), f32),) * heads)
        tops = score(c, tops, limit_of(c))
        for h in range(heads):
            top = jnp.max(tops[h], 0, keepdims=True)
            row_stats[0, h : h + 1, :] = jnp.sqrt(top + 1.0) * LOG2E

    def attend_weigh(c):
        tile = 32
        limit = limit_of(c)
        for h in range(heads):
            row_stats[1, h : h + 1, :] = jnp.zeros((1, rows), f32)

        def weigh(at, norms, limit):
            keep = key_row[:tile] + at <= limit
            fresh = []
            for h in range(heads):
                s = scores[h, band(at, tile), :]
                square = s * s + 1.0
                power = square * lax.rsqrt(square) * LOG2E - row_stats[0, h : h + 1, :]
                weight = jnp.exp2(jnp.where(keep, power, -1e30))
                scores[h, band(at, tile), :] = jnp.tanh(s) * weight
                fresh.append(norms[h] + fold(weight, jnp.sum))
            return tuple(fresh)

        def four(i, norms):
            for j in range(4):
                norms = weigh((4 * i + j) * tile, norms, limit)
            return norms

        norms = lax.fori_loop(
            0, (c + 1) * (rows // (4 * tile)), four, (jnp.zeros((8, rows), f32),) * heads
        )
        for h in range(heads):
            norm = jnp.sum(norms[h], 0, keepdims=True)
            row_stats[1, h : h + 1, :] = 1.0 / norm
            logsum_ref[c, h : h + 1, :] = row_stats[0, h : h + 1, :] + jnp.log(norm) * LOG2E

    def attend_mix(c):
        mixed_ref[4 * c + me] = jnp.zeros(mixed_ref.shape[1:], f32)

        def mix(kb, carry):
            for h in range(heads):
                mine = slice(h * HEAD_DIM, (h + 1) * HEAD_DIM)
                probs = scores[h, band(kb * rows, rows), :] * row_stats[1, h : h + 1, :]
                mixed_ref[4 * c + me, mine, :] += mm(vt_ref[kb, mine, :], probs.astype(bf16))
            return carry

        lax.fori_loop(0, c + 1, mix, 0)

    def attend_end(c):
        mixed_gather.start(c)
        own = mixed_ref[4 * c + me].astype(bf16)
        att_ref[c] = mm_nt(eye_rows, own).astype(bf16)

    def cast_merge():
        merge_gather.arrive()
        weight_squares[1] = jnp.zeros(weight_squares.shape[1:], f32)
        for owner in range(4):

            def cast(i, carry):
                block = middle[4 + merge_ref.shape[0] * owner + i]
                merge_low[band(owner * local + i * quarter, quarter), :] = block.astype(bf16)

                @pl.when(owner == me)
                def _():
                    weight_squares[1] += fold(block * block, jnp.sum)

                return carry

            lax.fori_loop(0, merge_ref.shape[0], cast, 0)

    def add_attended(c):
        mixed_gather.arrive(c)
        for owner in range(4):
            attended_cols[owner * local : (owner + 1) * local, :] = mixed_ref[
                4 * c + owner
            ].astype(bf16)
        out = mm_tn(attended_cols[...], merge_low[...])
        for i in range(4):
            rows_in = slice(i * quarter, (i + 1) * quarter)
            middle[4 * c + i] = part[4 * c + i] + out[rows_in]
        for half in range(2):
            middle_own[2 * c + half] = middle[4 * c + 2 * core + half]

    def feed(c):
        base = c * rows if deep else 0
        add_attended(c)
        load_cotangent(c).wait()

        def norm_tile(at):
            block, inside = 4 * c + at // quarter, band(lax.rem(at, quarter), 64)
            second[band(at, 64), :] = (normalize(middle[block, inside, :])[0] * gain_mid).astype(bf16)
            grad = mlp_part[block, inside, :] * live_rows(c * rows + at, 64)
            out_low[band(at, 64), :] = grad.astype(bf16)

        tiles(rows, 64, norm_tile)
        for half in range(2):
            block = 4 * c + 2 * core + half
            at = c * rows + (2 * core + half) * quarter
            middle[block] = mlp_part[block] * live_rows(at, quarter)
        mid_sum.store(c, mm(second[...], expand_low[...]))
        out_sum.store(c, mm_nt(out_low[...], shrink_low[...]))

        def gelu_tile(at):
            block, inside = 4 * c + at // quarter, band(lax.rem(at, quarter), 32)
            value = part[block, inside, :]
            square = value * value
            bend = jnp.tanh(GELU_A * value * (1.0 + GELU_B * square))
            half = 0.5 * (1.0 + bend)
            active[band(base + at, 32), :] = (value * half).astype(bf16)
            slope = half + 0.5 * value * (1.0 - bend * bend) * (
                GELU_A + (3.0 * GELU_A * GELU_B) * square
            )
            expand_back[band(base + at, 32), :] = (slope * mlp_part[block, inside, :]).astype(bf16)

        tiles(rows, 32, gelu_tile)
        here = band(base, rows)
        mid_sum.store(c, mm_nt(expand_back[here, :], expand_low[...]))
        mid_sum.start(c)
        out_sum.store(c, mm(active[here, :], shrink_low[...]))
        out_sum.start(c)
        if deep:
            lanes_here = band(c * rows, rows)
            second_cols[:, lanes_here] = second[...].T
            out_cols[:, lanes_here] = out_low[...].T
        else:
            for half in range(2):
                columns = slice(half * (width // 2), (half + 1) * (width // 2))
                add_slices(shrink_slices, half, mm_tn(out_low[:, columns], active[...]))
                add_slices(expand_slices, half, mm_tn(second[:, columns], expand_back[...]))

    def send_wide(scatter, p):
        if deep:
            left, right = (
                (out_cols, active) if scatter is shrink_scatter else (second_cols, expand_back)
            )
            at, size = scatter.pieces[p]
            columns = slice(at, at + size)
            for half in range(2):
                side = left[half * (width // 2) : (half + 1) * (width // 2), :]
                values = mm(side, right[:, columns])
                for i in range(scatter.count):
                    owner = half * scatter.count + i
                    scatter.slices[owner % 2, owner // 2, :, columns] = values[
                        i * share : (i + 1) * share
                    ]
        scatter.exchange(p).start()

    def finish_mid(values, c, half):
        normed, inv_dev = normalize(middle_own[2 * c + half])
        gain_two[...] += fold(values * normed, jnp.sum)
        upstream = middle[4 * c + 2 * core + half]
        return upstream + norm_back(values, gain_mid, normed, inv_dev)

    def finish_out(values, c, half):
        return middle_own[2 * c + half] + values

    def finish_in(values, c, half):
        normed, inv_dev = normalize(mid_chip[2 * c + half])
        gain_one[...] += fold(values * normed, jnp.sum)
        grad = middle[4 * c + 2 * core + half]
        return grad + norm_back(values, gain_in, normed, inv_dev)

    def attend_back_open(c):
        mid_sum.arrive(c)

        def low_tile(at):
            block, inside = 4 * c + at // quarter, band(lax.rem(at, quarter), 64)
            mid_low[band(at, 64), :] = middle[block, inside, :].astype(bf16)

        tiles(rows, 64, low_tile)
        merge_own_low = merge_low[band(me * local, local), :]
        back_rows[...] = mm_nt(mid_low[...], merge_own_low).astype(bf16)
        back_cols[...] = mm_nt(merge_own_low, mid_low[...]).astype(bf16)
        for half in range(2):
            columns = slice(half * (width // 2), (half + 1) * (width // 2))
            add_slices(merge_slices, half, mm_tn(mid_low[:, columns], att_ref[c]))

        for h in range(heads):
            queries[h] = jnp.where(head_row == h, qt_ref[c].astype(f32), 0.0).astype(bf16)
            columns = jnp.where(head_row == h, back_cols[...].astype(f32), 0.0)
            row_stats[2, h : h + 1, :] = jnp.sum(columns * mixed_ref[4 * c + me], 0, keepdims=True)
            grad_cols[h] = columns.astype(bf16)
            stack = slice(h * rows, (h + 1) * rows)
            query_rows[stack, :] = jnp.where(head_col == h, q_ref[c].astype(f32), 0.0).astype(bf16)
            grad_rows[stack, :] = jnp.where(head_col == h, back_rows[...].astype(f32), 0.0).astype(bf16)
        query_sum[...] = jnp.zeros_like(query_sum)

    def back_block(c, kb, diagonal):
        tile = 32
        limit = limit_of(c)
        for h in range(heads):
            scores[h, :rows, :] = mm(k_ref[kb], queries[h])
            scores[h, rows : 2 * rows, :] = mm(v_ref[kb], grad_cols[h])
        for h in range(heads):
            for i in range(rows // tile):
                at = slice(i * tile, (i + 1) * tile)
                skip = rows // 2 if diagonal and i * tile >= rows // 2 else 0
                s = scores[h, at, skip:]
                grad = scores[h, rows + i * tile : rows + (i + 1) * tile, skip:]
                square = s * s + 1.0
                inverse = lax.rsqrt(square)
                power = square * inverse * LOG2E - logsum_ref[c, h : h + 1, skip:]
                if diagonal:
                    keep = key_row[:tile] + (kb * rows + i * tile) <= limit[:, skip:]
                    power = jnp.where(keep, power, -1e30)
                weight = jnp.exp2(power)
                bend = jnp.tanh(s)
                slope = s * inverse
                pull = bend * grad
                change = grad + pull * (slope - bend) - slope * row_stats[2, h : h + 1, skip:]
                lanes = slice(h * rows + skip, (h + 1) * rows)
                probs_low[at, lanes] = (bend * weight).astype(bf16)
                score_low[at, lanes] = (weight * change).astype(bf16)
                if skip:
                    empty = slice(h * rows, h * rows + skip)
                    probs_low[at, empty] = jnp.zeros((tile, skip), bf16)
                    score_low[at, empty] = jnp.zeros((tile, skip), bf16)
        value_sum[kb] += mm(probs_low[...], grad_rows[...])
        key_sum[kb] += mm(score_low[...], query_rows[...])
        for h in range(heads):
            mine = slice(h * HEAD_DIM, (h + 1) * HEAD_DIM)
            query_sum[mine, :] += mm(kt_ref[kb, mine, :], score_low[:, h * rows : (h + 1) * rows])

    def attend_back(c, j):
        low, high = (c + 1) * j // 3, (c + 1) * (j + 1) // 3

        def one(kb, carry):
            back_block(c, kb, False)
            return carry

        lax.fori_loop(low, jnp.minimum(high, c), one, 0)

        @pl.when(j == 2)
        def _():
            back_block(c, c, True)

    def attend_back_end(c):
        query_low = (query_sum[...] * HEAD_DIM ** (-0.5)).astype(bf16)
        joint_back[:, :local] = mm_nt(eye_rows, query_low).astype(bf16)
        joint_back[:, local : 2 * local] = key_sum[c].astype(bf16)
        joint_back[:, 2 * local :] = value_sum[c].astype(bf16)
        in_sum.store(c, mm(joint_back[...], heads_low[...]))
        in_sum.start(c)
        for half in range(2):
            columns = slice(half * (width // 2), (half + 1) * (width // 2))
            add_slices(heads_slices, half, mm_tn(first_ref[c, :, columns], joint_back[...]))

    lanes = Gather(lane_box, lane_sems, "batch")
    sides = Gather(side_box, side_sems, "head")
    shares = Gather(share_box, share_sems, "head")
    squares = Gather(square_box, square_sems, "batch")
    square_shares = Gather(square_share, square_share_sems, "head")
    grads = (heads_own, merge_own, expand_own, shrink_own)
    row_lens = (width, width, width, head_count * shrink_own.shape[1])
    col_lens = (
        head_count * heads_own.shape[1],
        width,
        head_count * expand_own.shape[1],
        width,
    )
    on_side = (True, False, True, False)
    decay = 1.0 - STEP ** (-0.8)
    lane = lax.broadcasted_iota(jnp.int32, (1, width), 1)
    narrow = lax.broadcasted_iota(jnp.int32, (share, 128), 1)

    def whole_sum(values):
        return jnp.sum(jnp.sum(values, 0, keepdims=True), 1, keepdims=True)

    def clear():
        late = (heads_slices, merge_slices)
        for ref in late if deep else (expand_slices, shrink_slices, *late):

            def zero(i, carry):
                for parity in range(2):
                    ref[parity, i] = jnp.zeros(ref.shape[2:], f32)
                return carry

            lax.fori_loop(0, ref.shape[1], zero, 0)
        key_sum[...] = jnp.zeros_like(key_sum)
        value_sum[...] = jnp.zeros_like(value_sum)
        flat[...] = jnp.zeros_like(flat)
        for i, ref in enumerate((heads_rows, merge_cols, expand_rows, shrink_cols)):
            flat[i, :share] = ref[...]
        flat[...] = flat[...].T
        lane_old[...] = jnp.zeros_like(lane_old)
        for i in range(3):
            lane_old[0:1, i * local : (i + 1) * local] = heads_cols[i : i + 1, :]
        for i, ref in enumerate((merge_rows, expand_cols, shrink_rows)):
            lane_old[i + 1, : ref.shape[0]] = ref[...]
        lane_box[lanes.me] = jnp.zeros(lane_box.shape[1:], f32)
        side_box[sides.me] = jnp.zeros(side_box.shape[1:], f32)

    def statistics(i):
        square = grads[i][...] * grads[i][...]
        side_sum = jnp.sum(square, 1, keepdims=True)
        side_box[sides.me] = jnp.where(narrow == i, side_sum, side_box[sides.me])
        lane_box[lanes.me, i : i + 1, : square.shape[1]] = jnp.sum(square, 0, keepdims=True)

    def open_update():
        statistics(0)
        mine = lanes.me
        lane_box[mine, 4:5, :] = 0.5 * jnp.sum(gain_one[...], 0, keepdims=True)
        lane_box[mine, 5:6, :] = 0.5 * jnp.sum(gain_two[...], 0, keepdims=True)
        old = jnp.sum(flat[:share], 0, keepdims=True)
        lane_box[mine, 6:7, :] = pick(
            lane,
            [whole_sum(weight_squares[i]) / batch_count for i in range(4)]
            + [old[:, 0:1], old[:, 2:3]],
        )
        lanes.start()
        sides.start()

    def factors():
        total = lanes.total()
        lane_sum[...] = total
        mine = shares.me
        share_box[mine, 0:2, :] = total[4:6]
        share_box[mine, 2:3, :] = total[6:7] + pick(
            lane - 6,
            [jnp.sum(total[i : i + 1], 1, keepdims=True) for i in range(4)]
            + [jnp.sum(lane_old[i : i + 1, :], 1, keepdims=True) for i in (1, 3)],
        )
        share_box[mine, 3:8, :] = jnp.zeros((5, width), f32)
        shares.start()
        side_sum = sides.total()
        local_squares, side_factors, sides_new = [], [], []
        lane_next[...] = jnp.zeros_like(lane_next)
        lane_scale[...] = jnp.zeros_like(lane_scale)
        for i, grad in enumerate(grads):
            columns = grad.shape[1]
            side_len, lane_len = (
                (col_lens[i], row_lens[i]) if on_side[i] else (row_lens[i], col_lens[i])
            )
            side = decay * flat[:share, i : i + 1] + (1.0 - decay) * (
                side_sum[:, i : i + 1] / side_len + tiny_term
            )
            across = decay * lane_old[i : i + 1, :columns] + (1.0 - decay) * (
                lane_sum[i : i + 1, :columns] / lane_len + tiny_term
            )
            sides_new.append(side)
            lane_next[i : i + 1, :columns] = across
            side_factors.append(lax.rsqrt(side))
            lane_factor = lax.rsqrt(across)
            lane_scale[i : i + 1, :columns] = lane_factor
            update = grad[...] * side_factors[i] * lane_factor
            local_squares.append(whole_sum(update * update))
        side_next[...] = pick(narrow, sides_new)
        side_scale[...] = pick(narrow, side_factors)
        square_box[squares.me] = pick(
            lax.broadcasted_iota(jnp.int32, (8, 128), 1), local_squares
        )
        squares.start()

    def share_squares():
        share_sum[...] = shares.total()
        gain_grad = share_sum[0:2, :]
        gains_grad[...] = gain_grad
        moment_next[...] = decay * moment_ref[...] + (1.0 - decay) * (
            gain_grad * gain_grad + tiny_term
        )
        square_share[square_shares.me] = squares.total()
        square_shares.start()

    def close_update():
        scalar = [share_sum[2:3, i : i + 1] for i in range(12)]
        old_totals = (scalar[4] / head_count, scalar[10], scalar[5] / head_count, scalar[11])
        means = [
            decay * old_totals[i] / row_lens[i]
            + (1.0 - decay) * (scalar[6 + i] / (row_lens[i] * col_lens[i]) + tiny_term)
            for i in range(4)
        ]
        gain_step = gains_grad[...] * lax.rsqrt(moment_next[...])
        total = whole_sum(gain_step * gain_step)
        matrix_squares = square_shares.total()
        for i in range(4):
            total = total + means[i] * matrix_squares[0:1, i : i + 1]
        count = 4.0 * width * width + 2.0 * width * row_lens[3] + 2.0 * width
        rms = jnp.sqrt(total / count)
        rms_ref[...] = jnp.broadcast_to(rms, (8, 128))
        clip = 1.0 / jnp.maximum(1.0, rms / clip_level)
        side_scale[...] = side_scale[...] * pick(
            narrow[:1],
            [
                jnp.sqrt(means[i])
                * jnp.sqrt(scalar[i] / (1.0 * row_lens[i] * col_lens[i]))
                * clip
                for i in range(4)
            ],
        )
        gains = gains_ref[...]
        gains_next[...] = (
            gains - jnp.sqrt(jnp.mean(gains * gains, 1, keepdims=True)) * clip * gain_step
        )


    pieces = [(shrink_scatter, p, shrink_own) for p in range(len(shrink_pieces))]
    pieces += [(expand_scatter, p, expand_own) for p in range(len(expand_pieces))]
    pieces += [(merge_scatter, 0, merge_own)]
    pieces += [(heads_scatter, p, heads_own) for p in range(len(heads_pieces))]

    def step(u, carry):
        def at_chunk(name, action):
            at = STEPS[name]
            c = sum(jnp.where(u == at[i], i, 0) for i in range(1, 4))

            @pl.when((u == at[0]) | (u == at[1]) | (u == at[2]) | (u == at[3]))
            def _():
                action(c)

        def at_step(at, action):
            @pl.when(u == at)
            def _():
                action()

        def mix_and_send(c):
            attend_mix(c)
            attend_end(c)

        def cast_expand():
            wait_all(load_expand)
            cast_blocks(expand_ref.shape[0], expand_low, 2)
            start_all(load_shrink)

        def cast_shrink():
            wait_all(load_shrink)
            cast_blocks(shrink_ref.shape[0], shrink_low, 3)

        def back_first(c):
            attend_back_open(c)

            @pl.when(c == 0)
            def _():
                merge_scatter.start()

            attend_back(c, 0)

        def back_third(c):
            attend_back(c, 2)
            attend_back_end(c)

            @pl.when(c == 0)
            def _():
                heads_scatter.start()

        def finish_chunk(c):
            mid_sum.reduce_chip(c, finish_mid)
            load_own(c).start()

        def finish_inner(c):
            load_own(c).wait()
            in_sum.reduce_chip(c, finish_in)

        @pl.when(u <= STEPS["last_forward"])
        def _():
            at_chunk("project", project)
            at_chunk("score", attend_score)
            at_chunk("weigh", attend_weigh)
            at_chunk("mix", mix_and_send)
            at_chunk("attn_forward", mixed_gather.forward)
            at_step(STEPS["merge"][0], merge_gather.trade)
            at_step(STEPS["merge"][1], merge_gather.forward)
            at_step(STEPS["merge"][2], cast_merge)
            at_step(STEPS["cast"][0], cast_expand)
            at_step(STEPS["cast"][1], cast_shrink)
            at_step(STEPS["clear"], clear)
            at_chunk("feed", feed)

        @pl.when(u >= STEPS["first_backward"])
        def _():
            for i, (scatter, p, _) in enumerate(pieces[: len(STEPS["wide"])]):
                at_step(STEPS["wide"][i], partial(send_wide, scatter, p))
            at_chunk("mid_core", mid_sum.reduce_core)
            at_chunk("mid_chip", finish_chunk)
            at_chunk("back_first", back_first)
            at_chunk("back_second", lambda c: attend_back(c, 1))
            at_chunk("back_third", back_third)
            at_chunk("in_core", in_sum.reduce_core)
            for i, (scatter, p, out) in enumerate(pieces):
                at_step(STEPS["pair"][i], partial(scatter.reduce_pair, p))
            for i, (scatter, p, out) in enumerate(pieces):
                at_step(STEPS["rest"][i], partial(scatter.reduce_rest, out, p))
            for i, out in ((3, shrink_own), (2, expand_own), (1, merge_own)):
                ends = [at for at, piece in zip(STEPS["rest"], pieces) if piece[2] is out]
                at_step(max(ends), partial(statistics, i))
            at_chunk("out_core", out_sum.reduce_core)
            at_chunk("out_chip", lambda c: out_sum.reduce_chip(c, finish_out))
            at_chunk("in_chip", finish_inner)
            for at, action in zip(
                STEPS["update"], (open_update, factors, share_squares, close_update)
            ):
                at_step(at, action)
        return carry

    lax.fori_loop(0, STEPS["all"], step, 0)
    for scatter in scatters:
        scatter.settle()
    for gather in (lanes, sides, shares, squares, square_shares):
        gather.settle()
    each_chunk(out_sum.arrive)
    each_chunk(in_sum.arrive)


def run_layer(lengths, small, residual, cotangent, weights, batch_count, head_count):
    seq_len, width = residual.shape
    rows = CHUNK
    chunks, quarter = seq_len // rows, rows // 4
    local, wide = weights[1].shape[0], weights[3].shape[0]
    heads = local // HEAD_DIM
    count, share = batch_count // 2, width // batch_count
    deep = share % 8 == 0
    tokens = seq_len if deep else rows
    blocks = [m.reshape(-1, quarter, width) for m in (residual, cotangent, *weights)]
    whole = ((4 * chunks, quarter, width), f32)
    pair = ((2 * chunks, quarter, width), f32)
    row_low, col_low = ((chunks, rows, local), bf16), ((chunks, local, rows), bf16)
    low = ((rows, width), bf16)

    def scatter(columns):
        return [((count, share, columns), f32), ((max(count - 1, 1), share, columns), f32)]

    def slices(columns):
        return ((2, count, share, columns), f32)

    vm, hbm = pl.BlockSpec(memory_space=pltpu.VMEM), pl.BlockSpec(memory_space=pl.ANY)
    outs = [
        whole,
        whole,
        ((share, 3 * local), f32),
        ((share, local), f32),
        ((share, wide), f32),
        ((share, wide), f32),
        ((share, 128), f32),
        ((8, width), f32),
        ((share, 128), f32),
        ((8, width), f32),
        ((2, width), f32),
        ((2, width), f32),
        ((2, width), f32),
        ((8, 128), f32),
    ]
    scratch = [
        ((8, width), f32),
        ((8, width), f32),
        ((4, 8, width), f32),
        ((8, width), f32),
        ((8, width), f32),
        ((8, width), f32),
        ((128, 128), f32),
        ((batch_count, 8, width), f32),
        ((head_count, share, 128), f32),
        ((head_count, 8, width), f32),
        ((batch_count, 8, 128), f32),
        ((head_count, 8, 128), f32),
        ((3 * local, width), bf16),
        ((head_count * local, width), bf16),
        ((width, wide), bf16),
        ((wide, width), bf16),
        ((chunks, rows, width), bf16),
        row_low,
        row_low,
        row_low,
        col_low,
        col_low,
        col_low,
        ((head_count * chunks, local, rows), f32),
        row_low,
        ((chunks, 8, rows), f32),
        whole,
        whole,
        whole,
        *[pair] * 3,
        whole,
        pair,
        low,
        low,
        ((tokens, wide), bf16),
        ((tokens, wide), bf16),
        ((width, seq_len) if deep else (16, 128), bf16),
        ((width, seq_len) if deep else (16, 128), bf16),
        ((head_count * local, rows), bf16),
        low,
        ((rows, local), bf16),
        ((local, rows), bf16),
        ((rows, 3 * local), bf16),
        ((heads, local, rows), bf16),
        ((heads, local, rows), bf16),
        ((heads * rows, local), bf16),
        ((heads * rows, local), bf16),
        ((3, 8, rows), f32),
        ((heads, seq_len, rows), f32),
        ((rows, heads * rows), bf16),
        ((rows, heads * rows), bf16),
        ((chunks, rows, local), f32),
        ((chunks, rows, local), f32),
        ((local, rows), f32),
        slices(3 * local),
        slices(local),
        slices(wide),
        slices(wide),
        *scatter(3 * local),
        *scatter(local),
        *scatter(wide),
        *scatter(wide),
        pltpu.SemaphoreType.DMA((3 * chunks + 7,)),
        pltpu.SemaphoreType.DMA((5, 2, 4, chunks)),
        pltpu.SemaphoreType.DMA((4, 2, 5)),
        pltpu.SemaphoreType.DMA((4, 2, 5, max(count - 1, 1))),
        pltpu.SemaphoreType.DMA((2, batch_count)),
        pltpu.SemaphoreType.DMA((2, head_count)),
        pltpu.SemaphoreType.DMA((2, head_count)),
        pltpu.SemaphoreType.DMA((2, batch_count)),
        pltpu.SemaphoreType.DMA((2, head_count)),
    ]
    return pl.pallas_call(
        layer_kernel,
        out_shape=tuple(jax.ShapeDtypeStruct(*o) for o in outs),
        in_specs=[pl.BlockSpec(memory_space=pltpu.SMEM)] + [vm] * len(small) + [hbm] * 6,
        out_specs=(hbm, hbm) + (vm,) * 12,
        scratch_shapes=[pltpu.VMEM(*s) if isinstance(s, tuple) else s for s in scratch],
        compiler_params=pltpu.CompilerParams(
            collective_id=0, has_side_effects=True, vmem_limit_bytes=VMEM_LIMIT
        ),
        name="layer",
    )(lengths, *small, *blocks)


def apply_kernel(
    block_out,
    residual_grad,
    heads_weight,
    merge_weight,
    expand_weight,
    shrink_weight,
    heads_own,
    merge_own,
    expand_own,
    shrink_own,
    side_scale,
    lane_scale,
    side_new,
    lane_new,
    gains_grad,
    moment_new,
    gains_new,
    rms_new,
    block_out_ref,
    residual_grad_ref,
    heads_grad_ref,
    heads_rows_ref,
    heads_cols_ref,
    heads_next_ref,
    merge_grad_ref,
    merge_rows_ref,
    merge_cols_ref,
    merge_next_ref,
    expand_grad_ref,
    expand_rows_ref,
    expand_cols_ref,
    expand_next_ref,
    shrink_grad_ref,
    shrink_rows_ref,
    shrink_cols_ref,
    shrink_next_ref,
    gains_grad_ref,
    gain_moment_ref,
    gains_next_ref,
    rms_ref,
    window,
    master,
    rows_master,
    square,
    staged,
    sems,
):
    width = gains_grad.shape[1]
    share, local, wide = merge_own.shape[0], merge_own.shape[1], shrink_own.shape[1]
    me = lax.axis_index("batch")
    first = pl.multiple_of(jnp.minimum(me * share // 128 * 128, width - 256), 128)
    offset = me * share - first
    heads_at, merge_at = wide, wide + 3 * local
    copies = [
        pltpu.make_async_copy(shrink_weight.at[:, pl.ds(first, 256)], window.at[:wide], sems.at[0]),
        pltpu.make_async_copy(
            heads_weight.at[:, pl.ds(first, 256)], window.at[heads_at:merge_at], sems.at[1]
        ),
        pltpu.make_async_copy(
            merge_weight.at[:, pl.ds(first, 256)], window.at[merge_at:], sems.at[2]
        ),
        pltpu.make_async_copy(expand_weight.at[me], rows_master, sems.at[3]),
    ]
    blocks = block_out.shape[0] // 4
    through = []
    for part in range(4):
        for i, (src, dst) in enumerate(
            ((block_out, block_out_ref), (residual_grad, residual_grad_ref))
        ):
            rows = pl.ds(part * blocks, blocks)
            sem = 4 + 4 * part + 2 * i
            through.append(
                (
                    pltpu.make_async_copy(src.at[rows], staged.at[i, rows], sems.at[sem]),
                    pltpu.make_async_copy(staged.at[i, rows], dst.at[rows], sems.at[sem + 1]),
                )
            )
    for copy in copies:
        copy.start()
    for into, _ in through:
        into.start()
    gains_grad_ref[...] = gains_grad[...]
    gain_moment_ref[...] = moment_new[...]
    gains_next_ref[...] = gains_new[...]
    rms_ref[...] = rms_new[0:1, 0:1]
    expand_grad_ref[...] = expand_own[...]
    shrink_grad_ref[...] = shrink_own[...]
    for part in range(3):
        columns = slice(part * local, (part + 1) * local)
        heads_grad_ref[part] = heads_own[:, columns]
        heads_cols_ref[part : part + 1, :] = lane_new[0:1, columns]
    merge_rows_ref[...] = lane_new[1, :local]
    expand_cols_ref[...] = lane_new[2, :]
    shrink_rows_ref[...] = lane_new[3, :]
    square[:share, :128] = side_new[...]
    sides = square[:, :128].T
    heads_rows_ref[...] = sides[0, :share]
    merge_cols_ref[...] = sides[1, :share]
    expand_rows_ref[...] = sides[2, :share]
    shrink_cols_ref[...] = sides[3, :share]

    def step(i, own):
        columns = slice(0, own.shape[1])
        return own[...] * side_scale[:, i : i + 1] * lane_scale[i : i + 1, columns]

    square[:share, :local] = merge_own[...]
    merge_grad_ref[...] = square[...].T[:local, :share]
    square[:share, :local] = step(1, merge_own)
    for copy in copies:
        copy.wait()
    expand_next_ref[...] = rows_master[...] - step(2, expand_own)

    def turn(i, carry):
        rows = pl.ds(pl.multiple_of(i * 128, 128), 128)
        rolled = pltpu.roll(window[rows, :], 256 - offset, 1)
        window[rows, :] = rolled
        master[i] = rolled[:, :128].T
        return carry

    blocks_turned = window.shape[0] // 128
    lax.fori_loop(0, blocks_turned // 2, turn, 0)
    for into, out in through[:4]:
        into.wait()
        out.start()
    lax.fori_loop(blocks_turned // 2, blocks_turned, turn, 0)
    for into, out in through[4:]:
        into.wait()
        out.start()
    merge_next_ref[...] = window[merge_at:, :share] - square[...].T[:local, :share]

    shrink_step = step(3, shrink_own)
    for i in range(wide // 128):
        columns = slice(i * 128, (i + 1) * 128)
        shrink_next_ref[:, columns] = master[i, :share, :] - shrink_step[:, columns]
    heads_step = step(0, heads_own)
    heads_master = jnp.concatenate(
        [master[heads_at // 128 + i, :share, :] for i in range((3 * local + 127) // 128)], 1
    )
    for part in range(3):
        columns = slice(part * local, (part + 1) * local)
        heads_next_ref[part] = heads_master[:, columns] - heads_step[:, columns]
    for _, out in through:
        out.wait()


def run_apply(in_hbm, in_vmem, batch_count):
    block_out = in_hbm[0]
    heads_own, merge_own, expand_own, shrink_own = in_vmem[:4]
    width = in_vmem[8].shape[1]
    share, local, wide = merge_own.shape[0], merge_own.shape[1], shrink_own.shape[1]
    side, parts, pair = ((share,), f32), ((3, share, local), f32), ((2, width), f32)
    across, rows = ((local, share), f32), ((share, wide), f32)
    outs = [
        (block_out.shape, f32),
        (block_out.shape, f32),
        parts,
        side,
        ((3, local), f32),
        parts,
        across,
        ((local,), f32),
        side,
        across,
        rows,
        side,
        ((wide,), f32),
        rows,
        rows,
        ((wide,), f32),
        side,
        rows,
        pair,
        pair,
        pair,
        ((1, 1), f32),
    ]
    vm, hbm = pl.BlockSpec(memory_space=pltpu.VMEM), pl.BlockSpec(memory_space=pl.ANY)
    return pl.pallas_call(
        apply_kernel,
        out_shape=tuple(jax.ShapeDtypeStruct(*o) for o in outs),
        in_specs=[hbm] * len(in_hbm) + [vm] * len(in_vmem),
        out_specs=(hbm, hbm) + (vm,) * 20,
        scratch_shapes=[
            pltpu.VMEM((wide + 4 * local, 256), f32),
            pltpu.VMEM(((wide + 4 * local) // 128, 128, 128), f32),
            pltpu.VMEM((share, wide), f32),
            pltpu.VMEM((128, 256), f32),
            pltpu.VMEM((2, *block_out.shape), f32),
            pltpu.SemaphoreType.DMA((20,)),
        ],
        compiler_params=pltpu.CompilerParams(vmem_limit_bytes=VMEM_LIMIT),
        name="apply",
    )(*in_hbm, *in_vmem)


def body(
    residual,
    cotangent,
    lengths,
    gains,
    heads_weight,
    merge_weight,
    expand_weight,
    shrink_weight,
    gain_moment,
    heads_rows,
    heads_cols,
    merge_rows,
    merge_cols,
    expand_rows,
    expand_cols,
    shrink_rows,
    shrink_cols,
):
    seq_len, model_width = residual.shape
    local_width = merge_weight.shape[0]
    batch_count, head_count = lax.axis_size("batch"), lax.axis_size("head")
    heads_cols_w = jnp.transpose(heads_weight, (1, 2, 0)).reshape(3 * local_width, model_width)
    block_out, residual_grad, *shares = run_layer(
        lengths,
        [
            gains,
            gain_moment,
            heads_rows,
            heads_cols,
            merge_rows,
            merge_cols,
            expand_rows,
            expand_cols,
            shrink_rows,
            shrink_cols,
        ],
        residual,
        cotangent,
        (heads_cols_w, merge_weight, expand_weight, shrink_weight),
        batch_count,
        head_count,
    )
    outs = list(
        run_apply(
            [
                block_out,
                residual_grad,
                heads_cols_w,
                merge_weight,
                expand_weight.reshape(batch_count, model_width // batch_count, -1),
                shrink_weight,
            ],
            shares,
            batch_count,
        )
    )
    for i in (0, 1):
        outs[i] = outs[i].reshape(seq_len, model_width)
    for i in (2, 5):
        outs[i] = jnp.transpose(outs[i], (1, 0, 2))
    for i in (14, 17):
        outs[i] = outs[i].T
    outs[21] = outs[21].reshape(())
    return tuple(outs)


def solution(mesh):
    return jax.shard_map(
        body,
        mesh=mesh,
        in_specs=(
            P("batch", None),
            P("batch", None),
            P("batch"),
            P(),
            P(None, None, "head"),
            P("head", None),
            P(None, "head"),
            P("head", None),
            P(),
            P("batch"),
            P(None, "head"),
            P("head"),
            P("batch"),
            P("batch"),
            P("head"),
            P("head"),
            P("batch"),
        ),
        out_specs=(
            P("batch", None),
            P("batch", None),
            P("batch", None, "head"),
            P("batch"),
            P(None, "head"),
            P("batch", None, "head"),
            P("head", "batch"),
            P("head"),
            P("batch"),
            P("head", "batch"),
            P("batch", "head"),
            P("batch"),
            P("head"),
            P("batch", "head"),
            P("head", "batch"),
            P("head"),
            P("batch"),
            P("head", "batch"),
            P(),
            P(),
            P(),
            P(),
        ),
        check_vma=False,
    )
```

```python
from functools import partial

import jax
import jax.numpy as jnp
from jax import lax
from jax.experimental import pallas as pl
from jax.experimental.pallas import tpu as pltpu
from jax.sharding import PartitionSpec as P

HEAD_DIM = 64
FF = 3072
STEP = 10
CHUNK = 256

tiny_term = 1e-30
clip_level = 0.5
f32 = jnp.float32
bf16 = jnp.bfloat16
LOG2E = 1.4426950408889634
GELU_A = 0.7978845608028654
GELU_B = 0.044715
MESH = pl.DeviceIdType.MESH
VMEM_LIMIT = 63 * 1024 * 1024


def mm(a, b):
    return jnp.dot(a, b, preferred_element_type=f32)


def mm_nt(a, b):
    return lax.dot_general(a, b, (((1,), (1,)), ((), ())), preferred_element_type=f32)


def mm_tn(a, b):
    return lax.dot_general(a, b, (((0,), (0,)), ((), ())), preferred_element_type=f32)


def identity(size):
    rows = lax.broadcasted_iota(jnp.int32, (size, size), 0)
    return (rows == lax.broadcasted_iota(jnp.int32, (size, size), 1)).astype(bf16)


def band(start, size):
    return pl.ds(pl.multiple_of(start, size), size)


def tiles(total, rows, body):
    def step(i, carry):
        body(i * rows)
        return carry

    lax.fori_loop(0, total // rows, step, 0)


def cast_rows(src, dst, rows=64):
    def one(at):
        dst[band(at, rows), :] = src[band(at, rows), :].astype(bf16)

    tiles(src.shape[0], rows, one)


def fold(values, how):
    groups = values.reshape(values.shape[0] // 8, 8, values.shape[1])
    return how(groups, 0)


def normalize(values):
    center = values - jnp.mean(values, -1, keepdims=True)
    inv_dev = lax.rsqrt(jnp.mean(center * center, -1, keepdims=True) + 1e-05)
    return center * inv_dev, inv_dev


def norm_back(upstream, gain, normed, inv_dev):
    scaled = upstream * gain
    inner = (
        scaled
        - jnp.mean(scaled, -1, keepdims=True)
        - normed * jnp.mean(scaled * normed, -1, keepdims=True)
    )
    return inner * inv_dev


def head_place():
    me = lax.axis_index("head")
    core = lax.rem(me, 2)
    side = me // 2
    return core, side, me + 1 - 2 * core, me + 2 - 4 * side


def greet(peers):
    barrier = pltpu.get_barrier_semaphore()
    for peer in peers:
        pl.semaphore_signal(barrier, inc=1, device_id=peer, device_id_type=MESH)


def await_greetings(count):
    pl.semaphore_wait(pltpu.get_barrier_semaphore(), count)


STEPS = {
    "project": (0, 1, 3, 2),
    "score": (0, 6, 3, 4),
    "weigh": (1, 6, 3, 4),
    "mix": (1, 6, 3, 5),
    "attn_forward": (3, 8, 6, 7),
    "feed": (7, 10, 9, 8),
    "mid_core": (8, 11, 10, 9),
    "mid_chip": (11, 14, 12, 10),
    "back_first": (16, 15, 13, 11),
    "back_second": (16, 15, 14, 12),
    "back_third": (17, 15, 14, 12),
    "in_core": (18, 17, 15, 13),
    "in_chip": (19, 18, 17, 16),
    "out_core": (17, 14, 10, 18),
    "out_chip": (19, 17, 16, 21),
    "merge": (2, 4, 6),
    "cast": (0, 1),
    "clear": 5,
    "wide": (11, 14, 10, 13, 10, 13, 11),
    "pair": (12, 16, 10, 14, 11, 15, 13, 17, 17, 18, 18, 19, 19),
    "rest": (15, 20, 16, 19, 19, 17, 18, 18, 18, 20, 20, 20, 20),
    "update": (20, 20, 21, 21),
    "last_forward": 10,
    "first_backward": 8,
    "all": 22,
}


class Gather:
    def __init__(self, box, sems, axis):
        self.box, self.sems, self.axis = box, sems, axis
        self.count = box.shape[0]
        self.me = lax.axis_index(axis)

    def copy(self, k, slot):
        return pltpu.make_async_remote_copy(
            src_ref=self.box.at[slot],
            dst_ref=self.box.at[slot],
            send_sem=self.sems.at[0, k],
            recv_sem=self.sems.at[1, slot],
            device_id={self.axis: lax.rem(self.me + k, self.count)},
            device_id_type=MESH,
        )

    def each(self, action):
        def step(k, carry):
            action(k)
            return carry

        lax.fori_loop(1, self.count, step, 0)

    def start(self):
        self.each(lambda k: self.copy(k, self.me).start())

    def total(self):
        self.each(lambda k: self.copy(k, lax.rem(self.me + k, self.count)).wait_recv())
        return lax.fori_loop(
            1, self.count, lambda i, running: running + self.box[i], self.box[0]
        )

    def settle(self):
        self.each(lambda k: self.copy(k, self.me).wait_send())


def others(axis, count):
    me = lax.axis_index(axis)
    return [{axis: lax.rem(me + k, count)} for k in range(1, count)]


def pick(lane, values):
    row = jnp.zeros(lane.shape, f32)
    for at, value in enumerate(values):
        row = jnp.where(lane == at, value, row)
    return row


class HeadSum:
    def __init__(self, part, whole, from_core, from_chip, sems, place, home=False, chip_at=0):
        self.part, self.whole, self.home, self.chip_at = part, whole, home, chip_at
        self.from_core, self.from_chip, self.sems = from_core, from_chip, sems
        self.core, self.side, self.sibling, self.across = place

    def copy(self, src, dst, stage, c, peer):
        return pltpu.make_async_remote_copy(
            src_ref=src,
            dst_ref=dst,
            send_sem=self.sems.at[0, stage, c],
            recv_sem=self.sems.at[1, stage, c],
            device_id={"head": peer},
            device_id_type=MESH,
        )

    def pair(self, ref, c):
        return ref.at[pl.ds(2 * c, 2)]

    def mine(self, c):
        return self.whole.at[pl.ds(4 * c + 2 * self.core, 2)]

    def to_core(self, c):
        src = self.part.at[pl.ds(4 * c + 2 * (1 - self.core), 2)]
        return self.copy(src, self.pair(self.from_core, c), 0, c, self.sibling)

    def to_chip(self, c):
        return self.copy(
            self.pair(self.from_core, c),
            self.from_chip.at[pl.ds(self.chip_at + 2 * c, 2)],
            1,
            c,
            self.across,
        )

    def back_core(self, c):
        src = self.pair(self.from_core, c) if self.home else self.mine(c)
        return self.copy(src, self.mine(c), 2, c, self.sibling)

    def keep(self, c):
        return pltpu.make_async_copy(
            self.pair(self.from_core, c), self.mine(c), self.sems.at[0, 3, c]
        )

    def store(self, c, values):
        quarter = self.part.shape[1]
        for i in range(4):
            self.part[4 * c + i] = values[i * quarter : (i + 1) * quarter]

    def start(self, c):
        self.to_core(c).start()

    def reduce_core(self, c):
        self.to_core(c).wait()
        for half in range(2):
            self.from_core[2 * c + half] = (
                self.from_core[2 * c + half] + self.part[4 * c + 2 * self.core + half]
            )
        self.to_chip(c).start()

    def reduce_chip(self, c, finish):
        self.to_chip(c).wait()
        for half in range(2):
            total = self.from_core[2 * c + half] + self.from_chip[self.chip_at + 2 * c + half]
            result = finish(total, c, half)
            if self.home:
                self.from_core[2 * c + half] = result
            else:
                self.whole[4 * c + 2 * self.core + half] = result
        self.back_core(c).start()
        if self.home:
            self.keep(c).start()

    def arrive(self, c):
        self.back_core(c).wait()
        if self.home:
            self.keep(c).wait()


class HeadGather:
    def __init__(self, slot, sems, place):
        self.slot, self.sems = slot, sems
        self.core, self.side, self.sibling, self.across = place
        self.me = 2 * self.side + self.core

    def copy(self, stage, owner, c, peer):
        ref = self.slot(c, owner)
        return pltpu.make_async_remote_copy(
            src_ref=ref,
            dst_ref=ref,
            send_sem=self.sems.at[0, stage, c],
            recv_sem=self.sems.at[1, stage, c],
            device_id={"head": peer},
            device_id_type=MESH,
        )

    def over(self, c):
        return self.copy(0, self.me, c, self.across)

    def beside(self, c):
        return self.copy(1, self.me, c, self.sibling)

    def onward(self, c):
        return self.copy(2, self.across, c, self.sibling)

    def start(self, c):
        self.over(c).start()
        self.beside(c).start()

    def forward(self, c):
        self.over(c).wait_recv()
        self.onward(c).start()

    def arrive(self, c):
        self.over(c).wait_send()
        self.beside(c).wait()
        self.onward(c).wait()


class WeightGather:
    def __init__(self, slot, sems, place):
        self.slot, self.sems = slot, sems
        self.core, self.side, self.sibling, self.across = place
        self.me = 2 * self.side + self.core
        batch = lax.axis_index("batch")
        self.parity = lax.rem(batch, 2)
        self.pair = batch + 1 - 2 * self.parity

    def copy(self, stage, ref, device):
        return pltpu.make_async_remote_copy(
            src_ref=ref,
            dst_ref=ref,
            send_sem=self.sems.at[0, stage, 0],
            recv_sem=self.sems.at[1, stage, 0],
            device_id=device,
            device_id_type=MESH,
        )

    def half(self, owner):
        ref = self.slot(owner)
        columns = ref.shape[2] // 2
        return ref.at[:, :, pl.ds(pl.multiple_of(self.parity * columns, 128), columns)]

    def over(self):
        return self.copy(0, self.half(self.me), {"head": self.across})

    def beside(self):
        return self.copy(1, self.slot(self.me), {"head": self.sibling})

    def onward(self):
        return self.copy(2, self.slot(self.across), {"head": self.sibling})

    def swap(self):
        return self.copy(3, self.half(self.across), {"batch": self.pair})

    def start(self):
        self.over().start()
        self.beside().start()

    def trade(self):
        self.over().wait_recv()
        self.swap().start()

    def forward(self):
        self.swap().wait_recv()
        self.onward().start()

    def arrive(self):
        self.over().wait_send()
        self.swap().wait_send()
        self.beside().wait()
        self.onward().wait()


class BatchScatter:
    def __init__(self, slices, from_pair, from_rest, pair_sems, rest_sems, pieces):
        self.slices, self.from_pair, self.from_rest = slices, from_pair, from_rest
        self.pair_sems, self.rest_sems, self.pieces = pair_sems, rest_sems, pieces
        me = lax.axis_index("batch")
        self.parity, self.place = lax.rem(me, 2), me // 2
        self.pair = me + 1 - 2 * self.parity
        self.count = slices.shape[1]

    def exchange(self, p):
        columns = pl.ds(*self.pieces[p])
        return pltpu.make_async_remote_copy(
            src_ref=self.slices.at[1 - self.parity, :, :, columns],
            dst_ref=self.from_pair.at[:, :, columns],
            send_sem=self.pair_sems.at[0, p],
            recv_sem=self.pair_sems.at[1, p],
            device_id={"batch": self.pair},
            device_id_type=MESH,
        )

    def deliver(self, p, k):
        columns = pl.ds(*self.pieces[p])
        other = lax.rem(self.place + k, self.count)
        return pltpu.make_async_remote_copy(
            src_ref=self.from_pair.at[other, :, columns],
            dst_ref=self.from_rest.at[k - 1, :, columns],
            send_sem=self.rest_sems.at[0, p, k - 1],
            recv_sem=self.rest_sems.at[1, p, k - 1],
            device_id={"batch": other * 2 + self.parity},
            device_id_type=MESH,
        )

    def each(self, p, action):
        def step(k, carry):
            action(self.deliver(p, k))
            return carry

        lax.fori_loop(1, self.count, step, 0)

    def start(self):
        for p in range(len(self.pieces)):
            self.exchange(p).start()

    def reduce_pair(self, p):
        self.exchange(p).wait_recv()
        columns = pl.ds(*self.pieces[p])

        def step(i, carry):
            self.from_pair[i, :, columns] = (
                self.from_pair[i, :, columns] + self.slices[self.parity, i, :, columns]
            )
            return carry

        lax.fori_loop(0, self.count, step, 0)
        self.each(p, lambda copy: copy.start())

    def reduce_rest(self, out, p):
        self.each(p, lambda copy: copy.wait_recv())
        columns = pl.ds(*self.pieces[p])
        out[:, columns] = self.from_pair[self.place, :, columns]

        def step(k, carry):
            out[:, columns] += self.from_rest[k - 1, :, columns]
            return carry

        lax.fori_loop(1, self.count, step, 0)

    def settle(self):
        for p in range(len(self.pieces)):
            self.exchange(p).wait_send()
            self.each(p, lambda copy: copy.wait_send())


def add_slices(ref, half, values):
    count, share = ref.shape[1], ref.shape[2]
    for i in range(count):
        owner = half * count + i
        ref[owner % 2, owner // 2] += values[i * share : (i + 1) * share]


def layer_kernel(
    length_ref,
    gains_ref,
    moment_ref,
    heads_rows,
    heads_cols,
    merge_rows,
    merge_cols,
    expand_rows,
    expand_cols,
    shrink_rows,
    shrink_cols,
    residual_ref,
    cotangent_ref,
    heads_ref,
    merge_ref,
    expand_ref,
    shrink_ref,
    out_ref,
    in_grad_ref,
    heads_own,
    merge_own,
    expand_own,
    shrink_own,
    side_scale,
    lane_scale,
    side_next,
    lane_next,
    gains_grad,
    moment_next,
    gains_next,
    rms_ref,
    gain_one,
    gain_two,
    weight_squares,
    lane_old,
    lane_sum,
    share_sum,
    flat,
    lane_box,
    side_box,
    share_box,
    square_box,
    square_share,
    heads_low,
    merge_low,
    expand_low,
    shrink_low,
    first_ref,
    q_ref,
    k_ref,
    v_ref,
    qt_ref,
    kt_ref,
    vt_ref,
    mixed_ref,
    att_ref,
    logsum_ref,
    middle,
    part,
    mlp_part,
    from_core,
    from_chip,
    mid_chip,
    mlp_sums,
    middle_own,
    second,
    out_low,
    active,
    expand_back,
    second_cols,
    out_cols,
    attended_cols,
    mid_low,
    back_rows,
    back_cols,
    joint_back,
    queries,
    grad_cols,
    query_rows,
    grad_rows,
    row_stats,
    scores,
    probs_low,
    score_low,
    key_sum,
    value_sum,
    query_sum,
    heads_slices,
    merge_slices,
    expand_slices,
    shrink_slices,
    heads_pair,
    heads_rest,
    merge_pair,
    merge_rest,
    expand_pair,
    expand_rest,
    shrink_pair,
    shrink_rest,
    load_sems,
    sum_sems,
    pair_sems,
    rest_sems,
    lane_sems,
    side_sems,
    share_sems,
    square_sems,
    square_share_sems,
):
    chunks, rows, width = first_ref.shape
    quarter = rows // 4
    local = q_ref.shape[2]
    heads = local // HEAD_DIM
    last = chunks - 1
    place = head_place()
    core = place[0]
    me = 2 * place[1] + core

    def merge_slot(owner):
        count = merge_ref.shape[0]
        return middle.at[pl.ds(4 + count * owner, count)]

    merge_gather = WeightGather(merge_slot, sum_sems.at[4], place)
    mixed_gather = HeadGather(
        lambda c, owner: mixed_ref.at[4 * c + owner], sum_sems.at[0], place
    )
    mid_sum = HeadSum(part, middle, from_core, mid_chip, sum_sems.at[1], place)
    in_sum = HeadSum(part, in_grad_ref, from_core, from_chip, sum_sems.at[2], place, True)
    out_sum = HeadSum(
        mlp_part, out_ref, mlp_sums, mlp_sums, sum_sems.at[3], place, True, 2 * chunks
    )
    third = expand_slices.shape[3] // 3
    shrink_pieces = tuple((i * third, third) for i in range(3))
    expand_pieces = shrink_pieces[:2] + tuple((2 * third + i * third // 2, third // 2) for i in range(2))
    heads_pieces = tuple((at, min(128, 3 * local - at)) for at in range(0, 3 * local, 128))
    scatters = [
        BatchScatter(s, p, r, pair_sems.at[i], rest_sems.at[i], pieces)
        for i, (s, p, r, pieces) in enumerate(
            (
                (shrink_slices, shrink_pair, shrink_rest, shrink_pieces),
                (expand_slices, expand_pair, expand_rest, expand_pieces),
                (merge_slices, merge_pair, merge_rest, ((0, local),)),
                (heads_slices, heads_pair, heads_rest, heads_pieces),
            )
        )
    ]
    shrink_scatter, expand_scatter, merge_scatter, heads_scatter = scatters

    def load(src, dst, i):
        return pltpu.make_async_copy(src, dst, load_sems.at[i])

    def load_rows(c):
        return load(residual_ref.at[pl.ds(4 * c, 4)], part.at[pl.ds(4 * c, 4)], c)

    def load_cotangent(c):
        return load(
            cotangent_ref.at[pl.ds(4 * c, 4)], mlp_part.at[pl.ds(4 * c, 4)], chunks + c
        )

    def load_own(c):
        src = residual_ref.at[pl.ds(4 * c + 2 * core, 2)]
        return load(src, mid_chip.at[pl.ds(2 * c, 2)], 2 * chunks + c)

    run = 2 * chunks - 2

    def load_weight(src, i):
        count = src.shape[0]
        spans = ((0, 2, run), (run, 2 * chunks + 2, count - run))
        return [
            load(src.at[pl.ds(at, n)], mlp_sums.at[pl.ds(to, n)], 3 * chunks + 2 * i + half)
            for half, (at, to, n) in enumerate(spans)
        ]

    load_heads, load_expand, load_shrink = (
        load_weight(src, i) for i, src in enumerate((heads_ref, expand_ref, shrink_ref))
    )
    load_merge = load(merge_ref, merge_slot(me), 3 * chunks + 6)

    def start_all(copies):
        for copy in copies:
            copy.start()

    def wait_all(copies):
        for copy in copies:
            copy.wait()

    def each_chunk(action):
        def step(c, carry):
            action(c)
            return carry

        lax.fori_loop(0, chunks, step, 0)

    load_merge.start()
    start_all(load_heads)

    def open_loads(c):
        load_rows(c).start()
        load_cotangent(c).start()

    each_chunk(open_loads)
    share = heads_own.shape[0]
    deep = active.shape[0] > rows
    batch_count, head_count = lane_box.shape[0], side_box.shape[0]
    peers = others("batch", batch_count) + others("head", head_count)
    greet(peers)

    def cast_blocks(count, low, which):
        weight_squares[which] = jnp.zeros(weight_squares.shape[1:], f32)

        def step(i, carry):
            block = mlp_sums[2 + i + 2 * (i // run)]
            low[band(i * quarter, quarter), :] = block.astype(bf16)
            weight_squares[which] += fold(block * block, jnp.sum)
            return carry

        lax.fori_loop(0, count, step, 0)

    wait_all(load_heads)
    cast_blocks(heads_ref.shape[0], heads_low, 0)
    start_all(load_expand)
    load_merge.wait()
    await_greetings(len(peers))
    merge_gather.start()
    length = length_ref[0]
    gain_in, gain_mid = gains_ref[0:1, :], gains_ref[1:2, :]
    eye_local, eye_rows = identity(local), identity(rows)
    head_row = lax.broadcasted_iota(jnp.int32, (local, 1), 0) // HEAD_DIM
    head_col = lax.broadcasted_iota(jnp.int32, (1, local), 1) // HEAD_DIM
    key_row = lax.broadcasted_iota(jnp.int32, (rows, 1), 0)
    gain_one[...] = jnp.zeros_like(gain_one)
    gain_two[...] = jnp.zeros_like(gain_two)

    def live_rows(at, count):
        return (at + lax.broadcasted_iota(jnp.int32, (count, 1), 0) < length).astype(f32)

    def project(c):
        load_rows(c).wait()

        def norm_tile(at):
            values = part[4 * c + at // quarter, band(lax.rem(at, quarter), 64), :]
            first_ref[c, band(at, 64), :] = (normalize(values)[0] * gain_in).astype(bf16)

        tiles(rows, 64, norm_tile)
        normed = first_ref[c]
        live = live_rows(c * rows, rows)
        for which, (row_ref, col_ref) in enumerate(((q_ref, qt_ref), (k_ref, kt_ref), (v_ref, vt_ref))):
            joint = mm_nt(normed, heads_low[which * local : (which + 1) * local, :]).astype(bf16)
            scale = HEAD_DIM ** (-0.5) if which == 0 else live
            joint = (joint.astype(f32) * scale).astype(bf16)
            row_ref[c] = joint
            col_ref[c] = mm_nt(eye_local, joint).astype(bf16)

    def limit_of(c):
        return jnp.minimum(
            c * rows + lax.broadcasted_iota(jnp.int32, (1, rows), 1), length - 1
        )

    def attend_score(c):
        for h in range(heads):
            queries[h] = jnp.where(head_row == h, qt_ref[c].astype(f32), 0.0).astype(bf16)

        def score(kb, tops, limit=None):
            fresh = []
            for h in range(heads):
                s = mm(k_ref[kb], queries[h])
                scores[h, band(kb * rows, rows), :] = s
                square = s * s
                if limit is not None:
                    square = jnp.where(key_row + kb * rows <= limit, square, 0.0)
                fresh.append(jnp.maximum(tops[h], fold(square, jnp.max)))
            return tuple(fresh)

        tops = lax.fori_loop(0, c, score, (jnp.zeros((8, rows), f32),) * heads)
        tops = score(c, tops, limit_of(c))
        for h in range(heads):
            top = jnp.max(tops[h], 0, keepdims=True)
            row_stats[0, h : h + 1, :] = jnp.sqrt(top + 1.0) * LOG2E

    def attend_weigh(c):
        tile = 32
        limit = limit_of(c)
        for h in range(heads):
            row_stats[1, h : h + 1, :] = jnp.zeros((1, rows), f32)

        def weigh(at, norms, limit):
            keep = key_row[:tile] + at <= limit
            fresh = []
            for h in range(heads):
                s = scores[h, band(at, tile), :]
                square = s * s + 1.0
                power = square * lax.rsqrt(square) * LOG2E - row_stats[0, h : h + 1, :]
                weight = jnp.exp2(jnp.where(keep, power, -1e30))
                scores[h, band(at, tile), :] = jnp.tanh(s) * weight
                fresh.append(norms[h] + fold(weight, jnp.sum))
            return tuple(fresh)

        def four(i, norms):
            for j in range(4):
                norms = weigh((4 * i + j) * tile, norms, limit)
            return norms

        norms = lax.fori_loop(
            0, (c + 1) * (rows // (4 * tile)), four, (jnp.zeros((8, rows), f32),) * heads
        )
        for h in range(heads):
            norm = jnp.sum(norms[h], 0, keepdims=True)
            row_stats[1, h : h + 1, :] = 1.0 / norm
            logsum_ref[c, h : h + 1, :] = row_stats[0, h : h + 1, :] + jnp.log(norm) * LOG2E

    def attend_mix(c):
        mixed_ref[4 * c + me] = jnp.zeros(mixed_ref.shape[1:], f32)

        def mix(kb, carry):
            for h in range(heads):
                mine = slice(h * HEAD_DIM, (h + 1) * HEAD_DIM)
                probs = scores[h, band(kb * rows, rows), :] * row_stats[1, h : h + 1, :]
                mixed_ref[4 * c + me, mine, :] += mm(vt_ref[kb, mine, :], probs.astype(bf16))
            return carry

        lax.fori_loop(0, c + 1, mix, 0)

    def attend_end(c):
        mixed_gather.start(c)
        own = mixed_ref[4 * c + me].astype(bf16)
        att_ref[c] = mm_nt(eye_rows, own).astype(bf16)

    def cast_merge():
        merge_gather.arrive()
        weight_squares[1] = jnp.zeros(weight_squares.shape[1:], f32)
        for owner in range(4):

            def cast(i, carry):
                block = middle[4 + merge_ref.shape[0] * owner + i]
                merge_low[band(owner * local + i * quarter, quarter), :] = block.astype(bf16)

                @pl.when(owner == me)
                def _():
                    weight_squares[1] += fold(block * block, jnp.sum)

                return carry

            lax.fori_loop(0, merge_ref.shape[0], cast, 0)

    def add_attended(c):
        mixed_gather.arrive(c)
        for owner in range(4):
            attended_cols[owner * local : (owner + 1) * local, :] = mixed_ref[
                4 * c + owner
            ].astype(bf16)
        out = mm_tn(attended_cols[...], merge_low[...])
        for i in range(4):
            rows_in = slice(i * quarter, (i + 1) * quarter)
            middle[4 * c + i] = part[4 * c + i] + out[rows_in]
        for half in range(2):
            middle_own[2 * c + half] = middle[4 * c + 2 * core + half]

    def feed(c):
        base = c * rows if deep else 0
        add_attended(c)
        load_cotangent(c).wait()

        def norm_tile(at):
            block, inside = 4 * c + at // quarter, band(lax.rem(at, quarter), 64)
            second[band(at, 64), :] = (normalize(middle[block, inside, :])[0] * gain_mid).astype(bf16)
            grad = mlp_part[block, inside, :] * live_rows(c * rows + at, 64)
            out_low[band(at, 64), :] = grad.astype(bf16)

        tiles(rows, 64, norm_tile)
        for half in range(2):
            block = 4 * c + 2 * core + half
            at = c * rows + (2 * core + half) * quarter
            middle[block] = mlp_part[block] * live_rows(at, quarter)
        mid_sum.store(c, mm(second[...], expand_low[...]))
        out_sum.store(c, mm_nt(out_low[...], shrink_low[...]))

        def gelu_tile(at):
            block, inside = 4 * c + at // quarter, band(lax.rem(at, quarter), 32)
            value = part[block, inside, :]
            square = value * value
            bend = jnp.tanh(GELU_A * value * (1.0 + GELU_B * square))
            half = 0.5 * (1.0 + bend)
            active[band(base + at, 32), :] = (value * half).astype(bf16)
            slope = half + 0.5 * value * (1.0 - bend * bend) * (
                GELU_A + (3.0 * GELU_A * GELU_B) * square
            )
            expand_back[band(base + at, 32), :] = (slope * mlp_part[block, inside, :]).astype(bf16)

        tiles(rows, 32, gelu_tile)
        here = band(base, rows)
        mid_sum.store(c, mm_nt(expand_back[here, :], expand_low[...]))
        mid_sum.start(c)
        out_sum.store(c, mm(active[here, :], shrink_low[...]))
        out_sum.start(c)
        if deep:
            lanes_here = band(c * rows, rows)
            second_cols[:, lanes_here] = second[...].T
            out_cols[:, lanes_here] = out_low[...].T
        else:
            for half in range(2):
                columns = slice(half * (width // 2), (half + 1) * (width // 2))
                add_slices(shrink_slices, half, mm_tn(out_low[:, columns], active[...]))
                add_slices(expand_slices, half, mm_tn(second[:, columns], expand_back[...]))

    def send_wide(scatter, p):
        if deep:
            left, right = (
                (out_cols, active) if scatter is shrink_scatter else (second_cols, expand_back)
            )
            at, size = scatter.pieces[p]
            columns = slice(at, at + size)
            for half in range(2):
                side = left[half * (width // 2) : (half + 1) * (width // 2), :]
                values = mm(side, right[:, columns])
                for i in range(scatter.count):
                    owner = half * scatter.count + i
                    scatter.slices[owner % 2, owner // 2, :, columns] = values[
                        i * share : (i + 1) * share
                    ]
        scatter.exchange(p).start()

    def finish_mid(values, c, half):
        normed, inv_dev = normalize(middle_own[2 * c + half])
        gain_two[...] += fold(values * normed, jnp.sum)
        upstream = middle[4 * c + 2 * core + half]
        return upstream + norm_back(values, gain_mid, normed, inv_dev)

    def finish_out(values, c, half):
        return middle_own[2 * c + half] + values

    def finish_in(values, c, half):
        normed, inv_dev = normalize(mid_chip[2 * c + half])
        gain_one[...] += fold(values * normed, jnp.sum)
        grad = middle[4 * c + 2 * core + half]
        return grad + norm_back(values, gain_in, normed, inv_dev)

    def attend_back_open(c):
        mid_sum.arrive(c)

        def low_tile(at):
            block, inside = 4 * c + at // quarter, band(lax.rem(at, quarter), 64)
            mid_low[band(at, 64), :] = middle[block, inside, :].astype(bf16)

        tiles(rows, 64, low_tile)
        merge_own_low = merge_low[band(me * local, local), :]
        back_rows[...] = mm_nt(mid_low[...], merge_own_low).astype(bf16)
        back_cols[...] = mm_nt(merge_own_low, mid_low[...]).astype(bf16)
        for half in range(2):
            columns = slice(half * (width // 2), (half + 1) * (width // 2))
            add_slices(merge_slices, half, mm_tn(mid_low[:, columns], att_ref[c]))

        for h in range(heads):
            queries[h] = jnp.where(head_row == h, qt_ref[c].astype(f32), 0.0).astype(bf16)
            columns = jnp.where(head_row == h, back_cols[...].astype(f32), 0.0)
            row_stats[2, h : h + 1, :] = jnp.sum(columns * mixed_ref[4 * c + me], 0, keepdims=True)
            grad_cols[h] = columns.astype(bf16)
            stack = slice(h * rows, (h + 1) * rows)
            query_rows[stack, :] = jnp.where(head_col == h, q_ref[c].astype(f32), 0.0).astype(bf16)
            grad_rows[stack, :] = jnp.where(head_col == h, back_rows[...].astype(f32), 0.0).astype(bf16)
        query_sum[...] = jnp.zeros_like(query_sum)

    def back_block(c, kb, diagonal):
        tile = 32
        limit = limit_of(c)
        for h in range(heads):
            scores[h, :rows, :] = mm(k_ref[kb], queries[h])
            scores[h, rows : 2 * rows, :] = mm(v_ref[kb], grad_cols[h])
        for h in range(heads):
            for i in range(rows // tile):
                at = slice(i * tile, (i + 1) * tile)
                skip = rows // 2 if diagonal and i * tile >= rows // 2 else 0
                s = scores[h, at, skip:]
                grad = scores[h, rows + i * tile : rows + (i + 1) * tile, skip:]
                square = s * s + 1.0
                inverse = lax.rsqrt(square)
                power = square * inverse * LOG2E - logsum_ref[c, h : h + 1, skip:]
                if diagonal:
                    keep = key_row[:tile] + (kb * rows + i * tile) <= limit[:, skip:]
                    power = jnp.where(keep, power, -1e30)
                weight = jnp.exp2(power)
                bend = jnp.tanh(s)
                slope = s * inverse
                pull = bend * grad
                change = grad + pull * (slope - bend) - slope * row_stats[2, h : h + 1, skip:]
                lanes = slice(h * rows + skip, (h + 1) * rows)
                probs_low[at, lanes] = (bend * weight).astype(bf16)
                score_low[at, lanes] = (weight * change).astype(bf16)
                if skip:
                    empty = slice(h * rows, h * rows + skip)
                    probs_low[at, empty] = jnp.zeros((tile, skip), bf16)
                    score_low[at, empty] = jnp.zeros((tile, skip), bf16)
        value_sum[kb] += mm(probs_low[...], grad_rows[...])
        key_sum[kb] += mm(score_low[...], query_rows[...])
        for h in range(heads):
            mine = slice(h * HEAD_DIM, (h + 1) * HEAD_DIM)
            query_sum[mine, :] += mm(kt_ref[kb, mine, :], score_low[:, h * rows : (h + 1) * rows])

    def attend_back(c, j):
        low, high = (c + 1) * j // 3, (c + 1) * (j + 1) // 3

        def one(kb, carry):
            back_block(c, kb, False)
            return carry

        lax.fori_loop(low, jnp.minimum(high, c), one, 0)

        @pl.when(j == 2)
        def _():
            back_block(c, c, True)

    def attend_back_end(c):
        query_low = (query_sum[...] * HEAD_DIM ** (-0.5)).astype(bf16)
        joint_back[:, :local] = mm_nt(eye_rows, query_low).astype(bf16)
        joint_back[:, local : 2 * local] = key_sum[c].astype(bf16)
        joint_back[:, 2 * local :] = value_sum[c].astype(bf16)
        in_sum.store(c, mm(joint_back[...], heads_low[...]))
        in_sum.start(c)
        for half in range(2):
            columns = slice(half * (width // 2), (half + 1) * (width // 2))
            add_slices(heads_slices, half, mm_tn(first_ref[c, :, columns], joint_back[...]))

    lanes = Gather(lane_box, lane_sems, "batch")
    sides = Gather(side_box, side_sems, "head")
    shares = Gather(share_box, share_sems, "head")
    squares = Gather(square_box, square_sems, "batch")
    square_shares = Gather(square_share, square_share_sems, "head")
    grads = (heads_own, merge_own, expand_own, shrink_own)
    row_lens = (width, width, width, head_count * shrink_own.shape[1])
    col_lens = (
        head_count * heads_own.shape[1],
        width,
        head_count * expand_own.shape[1],
        width,
    )
    on_side = (True, False, True, False)
    decay = 1.0 - STEP ** (-0.8)
    lane = lax.broadcasted_iota(jnp.int32, (1, width), 1)
    narrow = lax.broadcasted_iota(jnp.int32, (share, 128), 1)

    def whole_sum(values):
        return jnp.sum(jnp.sum(values, 0, keepdims=True), 1, keepdims=True)

    def clear():
        late = (heads_slices, merge_slices)
        for ref in late if deep else (expand_slices, shrink_slices, *late):

            def zero(i, carry):
                for parity in range(2):
                    ref[parity, i] = jnp.zeros(ref.shape[2:], f32)
                return carry

            lax.fori_loop(0, ref.shape[1], zero, 0)
        key_sum[...] = jnp.zeros_like(key_sum)
        value_sum[...] = jnp.zeros_like(value_sum)
        flat[...] = jnp.zeros_like(flat)
        for i, ref in enumerate((heads_rows, merge_cols, expand_rows, shrink_cols)):
            flat[i, :share] = ref[...]
        flat[...] = flat[...].T
        lane_old[...] = jnp.zeros_like(lane_old)
        for i in range(3):
            lane_old[0:1, i * local : (i + 1) * local] = heads_cols[i : i + 1, :]
        for i, ref in enumerate((merge_rows, expand_cols, shrink_rows)):
            lane_old[i + 1, : ref.shape[0]] = ref[...]
        lane_box[lanes.me] = jnp.zeros(lane_box.shape[1:], f32)
        side_box[sides.me] = jnp.zeros(side_box.shape[1:], f32)

    def statistics(i):
        square = grads[i][...] * grads[i][...]
        side_sum = jnp.sum(square, 1, keepdims=True)
        side_box[sides.me] = jnp.where(narrow == i, side_sum, side_box[sides.me])
        lane_box[lanes.me, i : i + 1, : square.shape[1]] = jnp.sum(square, 0, keepdims=True)

    def open_update():
        statistics(0)
        mine = lanes.me
        lane_box[mine, 4:5, :] = 0.5 * jnp.sum(gain_one[...], 0, keepdims=True)
        lane_box[mine, 5:6, :] = 0.5 * jnp.sum(gain_two[...], 0, keepdims=True)
        old = jnp.sum(flat[:share], 0, keepdims=True)
        lane_box[mine, 6:7, :] = pick(
            lane,
            [whole_sum(weight_squares[i]) / batch_count for i in range(4)]
            + [old[:, 0:1], old[:, 2:3]],
        )
        lanes.start()
        sides.start()

    def factors():
        total = lanes.total()
        lane_sum[...] = total
        mine = shares.me
        share_box[mine, 0:2, :] = total[4:6]
        share_box[mine, 2:3, :] = total[6:7] + pick(
            lane - 6,
            [jnp.sum(total[i : i + 1], 1, keepdims=True) for i in range(4)]
            + [jnp.sum(lane_old[i : i + 1, :], 1, keepdims=True) for i in (1, 3)],
        )
        share_box[mine, 3:8, :] = jnp.zeros((5, width), f32)
        shares.start()
        side_sum = sides.total()
        local_squares, side_factors, sides_new = [], [], []
        lane_next[...] = jnp.zeros_like(lane_next)
        lane_scale[...] = jnp.zeros_like(lane_scale)
        for i, grad in enumerate(grads):
            columns = grad.shape[1]
            side_len, lane_len = (
                (col_lens[i], row_lens[i]) if on_side[i] else (row_lens[i], col_lens[i])
            )
            side = decay * flat[:share, i : i + 1] + (1.0 - decay) * (
                side_sum[:, i : i + 1] / side_len + tiny_term
            )
            across = decay * lane_old[i : i + 1, :columns] + (1.0 - decay) * (
                lane_sum[i : i + 1, :columns] / lane_len + tiny_term
            )
            sides_new.append(side)
            lane_next[i : i + 1, :columns] = across
            side_factors.append(lax.rsqrt(side))
            lane_factor = lax.rsqrt(across)
            lane_scale[i : i + 1, :columns] = lane_factor
            update = grad[...] * side_factors[i] * lane_factor
            local_squares.append(whole_sum(update * update))
        side_next[...] = pick(narrow, sides_new)
        side_scale[...] = pick(narrow, side_factors)
        square_box[squares.me] = pick(
            lax.broadcasted_iota(jnp.int32, (8, 128), 1), local_squares
        )
        squares.start()

    def share_squares():
        share_sum[...] = shares.total()
        gain_grad = share_sum[0:2, :]
        gains_grad[...] = gain_grad
        moment_next[...] = decay * moment_ref[...] + (1.0 - decay) * (
            gain_grad * gain_grad + tiny_term
        )
        square_share[square_shares.me] = squares.total()
        square_shares.start()

    def close_update():
        scalar = [share_sum[2:3, i : i + 1] for i in range(12)]
        old_totals = (scalar[4] / head_count, scalar[10], scalar[5] / head_count, scalar[11])
        means = [
            decay * old_totals[i] / row_lens[i]
            + (1.0 - decay) * (scalar[6 + i] / (row_lens[i] * col_lens[i]) + tiny_term)
            for i in range(4)
        ]
        gain_step = gains_grad[...] * lax.rsqrt(moment_next[...])
        total = whole_sum(gain_step * gain_step)
        matrix_squares = square_shares.total()
        for i in range(4):
            total = total + means[i] * matrix_squares[0:1, i : i + 1]
        count = 4.0 * width * width + 2.0 * width * row_lens[3] + 2.0 * width
        rms = jnp.sqrt(total / count)
        rms_ref[...] = jnp.broadcast_to(rms, (8, 128))
        clip = 1.0 / jnp.maximum(1.0, rms / clip_level)
        side_scale[...] = side_scale[...] * pick(
            narrow[:1],
            [
                jnp.sqrt(means[i])
                * jnp.sqrt(scalar[i] / (1.0 * row_lens[i] * col_lens[i]))
                * clip
                for i in range(4)
            ],
        )
        gains = gains_ref[...]
        gains_next[...] = (
            gains - jnp.sqrt(jnp.mean(gains * gains, 1, keepdims=True)) * clip * gain_step
        )


    pieces = [(shrink_scatter, p, shrink_own) for p in range(len(shrink_pieces))]
    pieces += [(expand_scatter, p, expand_own) for p in range(len(expand_pieces))]
    pieces += [(merge_scatter, 0, merge_own)]
    pieces += [(heads_scatter, p, heads_own) for p in range(len(heads_pieces))]

    def step(u, carry):
        def at_chunk(name, action):
            at = STEPS[name]
            c = sum(jnp.where(u == at[i], i, 0) for i in range(1, 4))

            @pl.when((u == at[0]) | (u == at[1]) | (u == at[2]) | (u == at[3]))
            def _():
                action(c)

        def at_step(at, action):
            @pl.when(u == at)
            def _():
                action()

        def mix_and_send(c):
            attend_mix(c)
            attend_end(c)

        def cast_expand():
            wait_all(load_expand)
            cast_blocks(expand_ref.shape[0], expand_low, 2)
            start_all(load_shrink)

        def cast_shrink():
            wait_all(load_shrink)
            cast_blocks(shrink_ref.shape[0], shrink_low, 3)

        def back_first(c):
            attend_back_open(c)

            @pl.when(c == 0)
            def _():
                merge_scatter.start()

            attend_back(c, 0)

        def back_third(c):
            attend_back(c, 2)
            attend_back_end(c)

            @pl.when(c == 0)
            def _():
                heads_scatter.start()

        def finish_chunk(c):
            mid_sum.reduce_chip(c, finish_mid)
            load_own(c).start()

        def finish_inner(c):
            load_own(c).wait()
            in_sum.reduce_chip(c, finish_in)

        @pl.when(u <= STEPS["last_forward"])
        def _():
            at_chunk("project", project)
            at_chunk("score", attend_score)
            at_chunk("weigh", attend_weigh)
            at_chunk("mix", mix_and_send)
            at_chunk("attn_forward", mixed_gather.forward)
            at_step(STEPS["merge"][0], merge_gather.trade)
            at_step(STEPS["merge"][1], merge_gather.forward)
            at_step(STEPS["merge"][2], cast_merge)
            at_step(STEPS["cast"][0], cast_expand)
            at_step(STEPS["cast"][1], cast_shrink)
            at_step(STEPS["clear"], clear)
            at_chunk("feed", feed)

        @pl.when(u >= STEPS["first_backward"])
        def _():
            for i, (scatter, p, _) in enumerate(pieces[: len(STEPS["wide"])]):
                at_step(STEPS["wide"][i], partial(send_wide, scatter, p))
            at_chunk("mid_core", mid_sum.reduce_core)
            at_chunk("mid_chip", finish_chunk)
            at_chunk("back_first", back_first)
            at_chunk("back_second", lambda c: attend_back(c, 1))
            at_chunk("back_third", back_third)
            at_chunk("in_core", in_sum.reduce_core)
            for i, (scatter, p, out) in enumerate(pieces):
                at_step(STEPS["pair"][i], partial(scatter.reduce_pair, p))
            for i, (scatter, p, out) in enumerate(pieces):
                at_step(STEPS["rest"][i], partial(scatter.reduce_rest, out, p))
            for i, out in ((3, shrink_own), (2, expand_own), (1, merge_own)):
                ends = [at for at, piece in zip(STEPS["rest"], pieces) if piece[2] is out]
                at_step(max(ends), partial(statistics, i))
            at_chunk("out_core", out_sum.reduce_core)
            at_chunk("out_chip", lambda c: out_sum.reduce_chip(c, finish_out))
            at_chunk("in_chip", finish_inner)
            for at, action in zip(
                STEPS["update"], (open_update, factors, share_squares, close_update)
            ):
                at_step(at, action)
        return carry

    lax.fori_loop(0, STEPS["all"], step, 0)
    for scatter in scatters:
        scatter.settle()
    for gather in (lanes, sides, shares, squares, square_shares):
        gather.settle()
    each_chunk(out_sum.arrive)
    each_chunk(in_sum.arrive)


def run_layer(lengths, small, residual, cotangent, weights, batch_count, head_count):
    seq_len, width = residual.shape
    rows = CHUNK
    chunks, quarter = seq_len // rows, rows // 4
    local, wide = weights[1].shape[0], weights[3].shape[0]
    heads = local // HEAD_DIM
    count, share = batch_count // 2, width // batch_count
    deep = share % 8 == 0
    tokens = seq_len if deep else rows
    blocks = [m.reshape(-1, quarter, width) for m in (residual, cotangent, *weights)]
    whole = ((4 * chunks, quarter, width), f32)
    pair = ((2 * chunks, quarter, width), f32)
    row_low, col_low = ((chunks, rows, local), bf16), ((chunks, local, rows), bf16)
    low = ((rows, width), bf16)

    def scatter(columns):
        return [((count, share, columns), f32), ((max(count - 1, 1), share, columns), f32)]

    def slices(columns):
        return ((2, count, share, columns), f32)

    vm, hbm = pl.BlockSpec(memory_space=pltpu.VMEM), pl.BlockSpec(memory_space=pl.ANY)
    outs = [
        whole,
        whole,
        ((share, 3 * local), f32),
        ((share, local), f32),
        ((share, wide), f32),
        ((share, wide), f32),
        ((share, 128), f32),
        ((8, width), f32),
        ((share, 128), f32),
        ((8, width), f32),
        ((2, width), f32),
        ((2, width), f32),
        ((2, width), f32),
        ((8, 128), f32),
    ]
    scratch = [
        ((8, width), f32),
        ((8, width), f32),
        ((4, 8, width), f32),
        ((8, width), f32),
        ((8, width), f32),
        ((8, width), f32),
        ((128, 128), f32),
        ((batch_count, 8, width), f32),
        ((head_count, share, 128), f32),
        ((head_count, 8, width), f32),
        ((batch_count, 8, 128), f32),
        ((head_count, 8, 128), f32),
        ((3 * local, width), bf16),
        ((head_count * local, width), bf16),
        ((width, wide), bf16),
        ((wide, width), bf16),
        ((chunks, rows, width), bf16),
        row_low,
        row_low,
        row_low,
        col_low,
        col_low,
        col_low,
        ((head_count * chunks, local, rows), f32),
        row_low,
        ((chunks, 8, rows), f32),
        whole,
        whole,
        whole,
        *[pair] * 3,
        whole,
        pair,
        low,
        low,
        ((tokens, wide), bf16),
        ((tokens, wide), bf16),
        ((width, seq_len) if deep else (16, 128), bf16),
        ((width, seq_len) if deep else (16, 128), bf16),
        ((head_count * local, rows), bf16),
        low,
        ((rows, local), bf16),
        ((local, rows), bf16),
        ((rows, 3 * local), bf16),
        ((heads, local, rows), bf16),
        ((heads, local, rows), bf16),
        ((heads * rows, local), bf16),
        ((heads * rows, local), bf16),
        ((3, 8, rows), f32),
        ((heads, seq_len, rows), f32),
        ((rows, heads * rows), bf16),
        ((rows, heads * rows), bf16),
        ((chunks, rows, local), f32),
        ((chunks, rows, local), f32),
        ((local, rows), f32),
        slices(3 * local),
        slices(local),
        slices(wide),
        slices(wide),
        *scatter(3 * local),
        *scatter(local),
        *scatter(wide),
        *scatter(wide),
        pltpu.SemaphoreType.DMA((3 * chunks + 7,)),
        pltpu.SemaphoreType.DMA((5, 2, 4, chunks)),
        pltpu.SemaphoreType.DMA((4, 2, 5)),
        pltpu.SemaphoreType.DMA((4, 2, 5, max(count - 1, 1))),
        pltpu.SemaphoreType.DMA((2, batch_count)),
        pltpu.SemaphoreType.DMA((2, head_count)),
        pltpu.SemaphoreType.DMA((2, head_count)),
        pltpu.SemaphoreType.DMA((2, batch_count)),
        pltpu.SemaphoreType.DMA((2, head_count)),
    ]
    return pl.pallas_call(
        layer_kernel,
        out_shape=tuple(jax.ShapeDtypeStruct(*o) for o in outs),
        in_specs=[pl.BlockSpec(memory_space=pltpu.SMEM)] + [vm] * len(small) + [hbm] * 6,
        out_specs=(hbm, hbm) + (vm,) * 12,
        scratch_shapes=[pltpu.VMEM(*s) if isinstance(s, tuple) else s for s in scratch],
        compiler_params=pltpu.CompilerParams(
            collective_id=0, has_side_effects=True, vmem_limit_bytes=VMEM_LIMIT
        ),
        name="layer",
    )(lengths, *small, *blocks)


def apply_kernel(
    block_out,
    residual_grad,
    heads_weight,
    merge_weight,
    expand_weight,
    shrink_weight,
    heads_own,
    merge_own,
    expand_own,
    shrink_own,
    side_scale,
    lane_scale,
    side_new,
    lane_new,
    gains_grad,
    moment_new,
    gains_new,
    rms_new,
    block_out_ref,
    residual_grad_ref,
    heads_grad_ref,
    heads_rows_ref,
    heads_cols_ref,
    heads_next_ref,
    merge_grad_ref,
    merge_rows_ref,
    merge_cols_ref,
    merge_next_ref,
    expand_grad_ref,
    expand_rows_ref,
    expand_cols_ref,
    expand_next_ref,
    shrink_grad_ref,
    shrink_rows_ref,
    shrink_cols_ref,
    shrink_next_ref,
    gains_grad_ref,
    gain_moment_ref,
    gains_next_ref,
    rms_ref,
    window,
    master,
    rows_master,
    square,
    staged,
    sems,
):
    width = gains_grad.shape[1]
    share, local, wide = merge_own.shape[0], merge_own.shape[1], shrink_own.shape[1]
    me = lax.axis_index("batch")
    first = pl.multiple_of(jnp.minimum(me * share // 128 * 128, width - 256), 128)
    offset = me * share - first
    heads_at, merge_at = wide, wide + 3 * local
    copies = [
        pltpu.make_async_copy(shrink_weight.at[:, pl.ds(first, 256)], window.at[:wide], sems.at[0]),
        pltpu.make_async_copy(
            heads_weight.at[:, pl.ds(first, 256)], window.at[heads_at:merge_at], sems.at[1]
        ),
        pltpu.make_async_copy(
            merge_weight.at[:, pl.ds(first, 256)], window.at[merge_at:], sems.at[2]
        ),
        pltpu.make_async_copy(expand_weight.at[me], rows_master, sems.at[3]),
    ]
    blocks = block_out.shape[0] // 4
    through = []
    for part in range(4):
        for i, (src, dst) in enumerate(
            ((block_out, block_out_ref), (residual_grad, residual_grad_ref))
        ):
            rows = pl.ds(part * blocks, blocks)
            sem = 4 + 4 * part + 2 * i
            through.append(
                (
                    pltpu.make_async_copy(src.at[rows], staged.at[i, rows], sems.at[sem]),
                    pltpu.make_async_copy(staged.at[i, rows], dst.at[rows], sems.at[sem + 1]),
                )
            )
    for copy in copies:
        copy.start()
    for into, _ in through:
        into.start()
    gains_grad_ref[...] = gains_grad[...]
    gain_moment_ref[...] = moment_new[...]
    gains_next_ref[...] = gains_new[...]
    rms_ref[...] = rms_new[0:1, 0:1]
    expand_grad_ref[...] = expand_own[...]
    shrink_grad_ref[...] = shrink_own[...]
    for part in range(3):
        columns = slice(part * local, (part + 1) * local)
        heads_grad_ref[part] = heads_own[:, columns]
        heads_cols_ref[part : part + 1, :] = lane_new[0:1, columns]
    merge_rows_ref[...] = lane_new[1, :local]
    expand_cols_ref[...] = lane_new[2, :]
    shrink_rows_ref[...] = lane_new[3, :]
    square[:share, :128] = side_new[...]
    sides = square[:, :128].T
    heads_rows_ref[...] = sides[0, :share]
    merge_cols_ref[...] = sides[1, :share]
    expand_rows_ref[...] = sides[2, :share]
    shrink_cols_ref[...] = sides[3, :share]

    def step(i, own):
        columns = slice(0, own.shape[1])
        return own[...] * side_scale[:, i : i + 1] * lane_scale[i : i + 1, columns]

    square[:share, :local] = merge_own[...]
    merge_grad_ref[...] = square[...].T[:local, :share]
    square[:share, :local] = step(1, merge_own)
    for copy in copies:
        copy.wait()
    expand_next_ref[...] = rows_master[...] - step(2, expand_own)

    def turn(i, carry):
        rows = pl.ds(pl.multiple_of(i * 128, 128), 128)
        rolled = pltpu.roll(window[rows, :], 256 - offset, 1)
        window[rows, :] = rolled
        master[i] = rolled[:, :128].T
        return carry

    blocks_turned = window.shape[0] // 128
    lax.fori_loop(0, blocks_turned // 2, turn, 0)
    for into, out in through[:4]:
        into.wait()
        out.start()
    lax.fori_loop(blocks_turned // 2, blocks_turned, turn, 0)
    for into, out in through[4:]:
        into.wait()
        out.start()
    merge_next_ref[...] = window[merge_at:, :share] - square[...].T[:local, :share]

    shrink_step = step(3, shrink_own)
    for i in range(wide // 128):
        columns = slice(i * 128, (i + 1) * 128)
        shrink_next_ref[:, columns] = master[i, :share, :] - shrink_step[:, columns]
    heads_step = step(0, heads_own)
    heads_master = jnp.concatenate(
        [master[heads_at // 128 + i, :share, :] for i in range((3 * local + 127) // 128)], 1
    )
    for part in range(3):
        columns = slice(part * local, (part + 1) * local)
        heads_next_ref[part] = heads_master[:, columns] - heads_step[:, columns]
    for _, out in through:
        out.wait()


def run_apply(in_hbm, in_vmem, batch_count):
    block_out = in_hbm[0]
    heads_own, merge_own, expand_own, shrink_own = in_vmem[:4]
    width = in_vmem[8].shape[1]
    share, local, wide = merge_own.shape[0], merge_own.shape[1], shrink_own.shape[1]
    side, parts, pair = ((share,), f32), ((3, share, local), f32), ((2, width), f32)
    across, rows = ((local, share), f32), ((share, wide), f32)
    outs = [
        (block_out.shape, f32),
        (block_out.shape, f32),
        parts,
        side,
        ((3, local), f32),
        parts,
        across,
        ((local,), f32),
        side,
        across,
        rows,
        side,
        ((wide,), f32),
        rows,
        rows,
        ((wide,), f32),
        side,
        rows,
        pair,
        pair,
        pair,
        ((1, 1), f32),
    ]
    vm, hbm = pl.BlockSpec(memory_space=pltpu.VMEM), pl.BlockSpec(memory_space=pl.ANY)
    return pl.pallas_call(
        apply_kernel,
        out_shape=tuple(jax.ShapeDtypeStruct(*o) for o in outs),
        in_specs=[hbm] * len(in_hbm) + [vm] * len(in_vmem),
        out_specs=(hbm, hbm) + (vm,) * 20,
        scratch_shapes=[
            pltpu.VMEM((wide + 4 * local, 256), f32),
            pltpu.VMEM(((wide + 4 * local) // 128, 128, 128), f32),
            pltpu.VMEM((share, wide), f32),
            pltpu.VMEM((128, 256), f32),
            pltpu.VMEM((2, *block_out.shape), f32),
            pltpu.SemaphoreType.DMA((20,)),
        ],
        compiler_params=pltpu.CompilerParams(vmem_limit_bytes=VMEM_LIMIT),
        name="apply",
    )(*in_hbm, *in_vmem)


def body(
    residual,
    cotangent,
    lengths,
    gains,
    heads_weight,
    merge_weight,
    expand_weight,
    shrink_weight,
    gain_moment,
    heads_rows,
    heads_cols,
    merge_rows,
    merge_cols,
    expand_rows,
    expand_cols,
    shrink_rows,
    shrink_cols,
):
    seq_len, model_width = residual.shape
    local_width = merge_weight.shape[0]
    batch_count, head_count = lax.axis_size("batch"), lax.axis_size("head")
    heads_cols_w = jnp.transpose(heads_weight, (1, 2, 0)).reshape(3 * local_width, model_width)
    block_out, residual_grad, *shares = run_layer(
        lengths,
        [
            gains,
            gain_moment,
            heads_rows,
            heads_cols,
            merge_rows,
            merge_cols,
            expand_rows,
            expand_cols,
            shrink_rows,
            shrink_cols,
        ],
        residual,
        cotangent,
        (heads_cols_w, merge_weight, expand_weight, shrink_weight),
        batch_count,
        head_count,
    )
    outs = list(
        run_apply(
            [
                block_out,
                residual_grad,
                heads_cols_w,
                merge_weight,
                expand_weight.reshape(batch_count, model_width // batch_count, -1),
                shrink_weight,
            ],
            shares,
            batch_count,
        )
    )
    for i in (0, 1):
        outs[i] = outs[i].reshape(seq_len, model_width)
    for i in (2, 5):
        outs[i] = jnp.transpose(outs[i], (1, 0, 2))
    for i in (14, 17):
        outs[i] = outs[i].T
    outs[21] = outs[21].reshape(())
    return tuple(outs)


def solution(mesh):
    return jax.shard_map(
        body,
        mesh=mesh,
        in_specs=(
            P("batch", None),
            P("batch", None),
            P("batch"),
            P(),
            P(None, None, "head"),
            P("head", None),
            P(None, "head"),
            P("head", None),
            P(),
            P("batch"),
            P(None, "head"),
            P("head"),
            P("batch"),
            P("batch"),
            P("head"),
            P("head"),
            P("batch"),
        ),
        out_specs=(
            P("batch", None),
            P("batch", None),
            P("batch", None, "head"),
            P("batch"),
            P(None, "head"),
            P("batch", None, "head"),
            P("head", "batch"),
            P("head"),
            P("batch"),
            P("head", "batch"),
            P("batch", "head"),
            P("batch"),
            P("head"),
            P("batch", "head"),
            P("head", "batch"),
            P("head"),
            P("batch"),
            P("head", "batch"),
            P(),
            P(),
            P(),
            P(),
        ),
        check_vma=False,
    )
```
